256 devices in a mesh: task: 32 (over x, z_hi, core), tensor: 8 (over z_lo, y).
Axes of the slice: x: 4, y: 4, z: 8 (z_hi: 4, z_lo: 2; z = z_hi * 2 + z_lo), core: 2. Of those that a mesh axis runs over, the one named last changes fastest.
Arguments:
- tokens: bfloat16 [256, 8192], P('task', 'tensor'), may hold values from -6 to 6
- router: float32 [256, 16], P('task'), may hold values from 0 to 1
- gate_up_weight: bfloat16 [2, 8192, 29568], P(None, 'task', 'tensor'), may hold values from -0.0625 to 0.0625
- down_weight: bfloat16 [29568, 8192], P('tensor', 'task'), may hold values from -0.03125 to 0.03125
- lower_factor: bfloat16 [2, 8192, 4096], P(None, 'tensor', 'task'), may hold values from -0.0625 to 0.0625
- upper_factor: bfloat16 [2, 4096, 29568], P(None, 'task', 'tensor'), may hold values from -0.09375 to 0.09375
Outputs:
- mixed: float32 [256, 8192], P('tensor', 'task')
The draws below stay inside these ranges and needn't reach their ends.
All inputs are finite; a program needn't handle non-finite values.
Results may differ from the reference program's by a relative error of at most 0.015.
Values may be sent and summed in bfloat16 or wider, within the bound.
No kernel may reach another device: no remote copies, remote signals or barrier semaphores. Data moves between devices by JAX's collectives and lax.ppermute only.
A program may use at most 64 MiB of HBM per device.

```python
import jax
import jax.numpy as jnp

D = 8192
FF = 29568
TASKS = 16
RANK = 256
TOKENS = 256


def block_levels(stream_key, extent, shards, least, high):
    def one(dim, parts):
        heights = jax.random.uniform(jax.random.fold_in(jax.random.fold_in(stream_key, 6), dim), (parts,), jnp.float32, least / len(shards), high / len(shards))
        return jnp.repeat(jnp.exp(heights), extent[dim] // parts).reshape((-1,) + (1,) * (len(extent) - dim - 1))

    gain = one(*shards[0])
    for cut in shards[1:]:
        gain = gain * one(*cut)
    return gain


def scatter_about(key, extent, scale, most, shards=(), held_as=jnp.bfloat16):
    drawn = scale * jax.random.normal(key, extent, jnp.float32)
    if shards:
        drawn = drawn * block_levels(key, extent, shards, -0.22, 0.18)
    return jnp.clip(drawn, -most, most).astype(held_as)


def setup_inputs(seed: int = 0) -> dict:
    splits = jax.random.split(jax.random.key(seed), 7)
    return {
        "tokens": scatter_about(splits[0], (TOKENS, D), 1.0, 6.0, ((0, 32), (1, 8))),
        "router": jnp.clip(1.0 * jax.random.uniform(splits[1], (TOKENS, TASKS), jnp.float32) ** block_levels(splits[1], (TOKENS, TASKS), ((0, 32),), -0.2, 0.2), 0.0, 1.0),
        "gate_up_weight": scatter_about(splits[2], (2, D, FF), D ** -0.5, 0.0625, ((1, 32), (2, 8))),
        "down_weight": scatter_about(splits[3], (FF, D), FF ** -0.5, 0.03125, ((0, 8), (1, 32))),
        "lower_factor": scatter_about(splits[4], (2, D, TASKS * RANK), D ** -0.5, 0.0625, ((1, 8), (2, 32))),
        "upper_factor": scatter_about(splits[5], (2, TASKS * RANK, FF), (TASKS * RANK) ** -0.5, 0.09375, ((1, 32), (2, 8))),
    }


def reference(tokens, router, gate_up_weight, down_weight, lower_factor, upper_factor):
    task_of = (jnp.arange(TASKS * RANK) // RANK).astype(jnp.int32)
    task_scale = router[:, task_of]
    outputs = []
    for branch in range(2):
        latent = jnp.dot(tokens, lower_factor[branch], preferred_element_type=jnp.float32)
        scaled = (latent * task_scale).astype(jnp.bfloat16)
        shared = jnp.dot(tokens, gate_up_weight[branch], preferred_element_type=jnp.float32)
        outputs.append(shared + jnp.dot(scaled, upper_factor[branch], preferred_element_type=jnp.float32))
    hidden = (jax.nn.silu(outputs[0]) * outputs[1]).astype(jnp.bfloat16)
    return jnp.dot(hidden, down_weight, preferred_element_type=jnp.float32).astype(jnp.float32)
```

```python
import functools

import jax
import jax.numpy as jnp
from jax import lax
from jax.experimental import pallas as pl
from jax.experimental.pallas import tpu as pltpu
from jax.sharding import PartitionSpec as P

F32 = jnp.float32
BF16 = jnp.bfloat16
TASKS = 16
NX, NZ, NC = 4, 4, 2
NQ = NX * NZ
VMEM_BYTES = 48 * 1024 * 1024


def task_of(x, z, c):
    return (x * NZ + z) * NC + c


def task_perm(move):
    pairs = []
    for x in range(NX):
        for z in range(NZ):
            for c in range(NC):
                pairs.append((task_of(x, z, c), task_of(*move(x, z, c))))
    return pairs


CORE = task_perm(lambda x, z, c: (x, z, 1 - c))
TO_X = {d: task_perm(lambda x, z, c, d=d: ((x + d) % NX, z, c)) for d in (1, 2, 3)}
TO_Z = {d: task_perm(lambda x, z, c, d=d: (x, (z + d) % NZ, c)) for d in (1, 2, 3)}
CHIPS = [[task_of(x, z, c) for x in range(NX) for z in range(NZ)] for c in range(NC)]


def call(kernel, out_shape, *args, scalars, **kw):
    return pl.pallas_call(
        kernel,
        out_shape=out_shape,
        grid_spec=pltpu.PrefetchScalarGridSpec(num_scalar_prefetch=1, **kw),
        compiler_params=pltpu.CompilerParams(vmem_limit_bytes=VMEM_BYTES),
    )(scalars, *args)


def whole(a):
    return pl.BlockSpec(a.shape, lambda *_: (0,) * len(a.shape))


def simple(kernel, out_shape, *args, scalars):
    outs = out_shape if isinstance(out_shape, (list, tuple)) else [out_shape]
    specs = [whole(o) for o in outs]
    return call(
        kernel,
        out_shape,
        *args,
        scalars=scalars,
        grid=(1,),
        in_specs=[whole(a) for a in args],
        out_specs=specs if isinstance(out_shape, (list, tuple)) else specs[0],
    )


def latent_kernel(width, s, own, other, low_own, low_other, out):
    q = s[3]

    def rows(ref):
        v = ref[...].astype(F32)
        return v.reshape(v.shape[0] * v.shape[1], v.shape[2])

    x = jnp.concatenate([rows(own), rows(other)], axis=0)
    low = jnp.concatenate([low_own[0], low_other[...]], axis=1)
    lat = jnp.dot(x[:, :width].astype(BF16), low, preferred_element_type=F32)
    tail = x[:, width:]
    lane = lax.broadcasted_iota(jnp.int32, tail.shape, 1)
    weight = jnp.sum(
        jnp.where((lane == q) | (lane == TASKS + q), tail, 0.0), axis=1, keepdims=True
    )
    lat = lat * weight
    ranks = lat.shape[1]
    lat = lat.reshape(2, own.shape[0], own.shape[1], ranks)
    out[:, :, :ranks] = jnp.concatenate([lat[0], lat[1]], axis=1).astype(BF16)
    feats = out.shape[2] - ranks
    start = pl.multiple_of(lax.rem(q, 2) * feats, feats)
    part = [r[:, :, pl.ds(start, feats)].astype(F32) for r in (own, other)]
    out[:, :, ranks:] = jnp.concatenate(part, axis=1).astype(BF16)


def mid_kernel(ranks, s, got, out):
    total = jnp.sum(got[:, :, :ranks].astype(F32), axis=0).astype(BF16)
    feats = got[s[3] // 2, :, ranks:]
    for j in range(out.shape[0]):
        out[j, :, :ranks] = total
        out[j, :, ranks:] = feats


def main_kernel(ranks, s, got, w_own, w_other, u_own, u_other, o0, o1, o2, o3, rows):
    x, z, c = s[0], s[1], s[2]
    half = (rows.shape[1] - ranks) // 2

    @pl.when(pl.program_id(0) == 0)
    def _():
        a = pl.multiple_of(ranks + c * half, half)
        b = pl.multiple_of(ranks + (1 - c) * half, half)
        for dx in range(NX):
            for dz in range(NZ):
                q = lax.rem(x + dx, NX) * NZ + lax.rem(z + dz, NZ)
                at = pl.ds(16 * (dx * NZ + dz), 16)
                rows[at, :half] = got[q, :, pl.ds(a, half)]
                rows[at, half : 2 * half] = got[q, :, pl.ds(b, half)]
                rows[at, 2 * half :] = got[q, :, :ranks]

    w = jnp.concatenate([w_own[0], w_other[...], u_own[0], u_other[...]], axis=0)
    p = jnp.dot(rows[...], w, preferred_element_type=F32)
    m = o0.shape[0]
    o0[...] = p[:m]
    o1[...] = p[m : 2 * m].astype(BF16)
    o2[...] = p[2 * m : 3 * m].astype(BF16)
    o3[...] = p[3 * m :].astype(BF16)


def x_sum_kernel(s, a0, a1, a2, a3, o0, o1, o2, o3):
    m = o0.shape[0]
    for i, o in enumerate((o0, o1, o2, o3)):
        at = pl.ds(i * m, m)
        t = a0[at] + a1[at].astype(F32) + a2[at].astype(F32) + a3[at].astype(F32)
        o[...] = t.astype(o.dtype)


def z_sum_kernel(s, a0, a1, a2, a3, keep, send):
    t = a0[...] + a1[...].astype(F32) + a2[...].astype(F32) + a3[...].astype(F32)
    m = keep.shape[0]
    keep[...] = t[:m]
    send[...] = t[m:]


def silu_kernel(s, keep, got, out):
    first = s[2] == 0
    gate = jnp.where(first, keep[...], got[...])
    up = jnp.where(first, got[...], keep[...])
    out[...] = (gate / (1.0 + jnp.exp(-gate)) * up).astype(BF16)


def down_kernel(s, h0, h1, h2, h3, w_own, w_other, out):
    x, z = s[0], s[1]
    h = jnp.concatenate([h0[...], h1[...], h2[...], h3[...]], axis=0)
    half = w_own.shape[1]
    for k, w in enumerate((w_own, w_other)):
        p = jnp.dot(h, w[...], preferred_element_type=F32)
        for dx in range(NX):
            for dz in range(NZ):
                q = lax.rem(x - dx + NX, NX) * NZ + lax.rem(z - dz + NZ, NZ)
                r = 8 * (dx * NZ + dz)
                out[q, :, half * k : half * (k + 1)] = p[r : r + 8].astype(out.dtype)


def out_sum_kernel(s, got, keep, send):
    t = jnp.sum(got[...].astype(F32), axis=0)
    half = keep.shape[-1]
    keep[...] = t[..., :half]
    send[...] = t[..., half:]


def on_device(tokens, router, gate_up_weight, down_weight, lower_factor, upper_factor):
    t = lax.axis_index("task").astype(jnp.int32)
    c = lax.rem(t, NC)
    q = t // NC
    x, z = q // NZ, lax.rem(q, NZ)
    s = jnp.stack([x, z, c, q])
    tensor = lax.axis_size("tensor")

    def permute(a, perm):
        return lax.ppermute(a, "task", perm)

    def sds(shape, dtype=BF16):
        return jax.ShapeDtypeStruct(shape, dtype)

    def other(a):
        return lax.dynamic_index_in_dim(a, 1 - c, 0, keepdims=False)

    def own_spec(a, block=None):
        return pl.BlockSpec((1, a.shape[1], block or a.shape[2]), lambda i, s: (s[2], 0, i))

    rows, width = tokens.shape
    ranks = 2 * lower_factor.shape[2]
    feats = 2 * gate_up_weight.shape[1]
    hid = gate_up_weight.shape[2]

    low_other = permute(other(lower_factor), CORE)
    w_other = permute(other(gate_up_weight), CORE)
    u_other = permute(other(upper_factor), CORE)
    down_other = permute(down_weight, CORE)

    high = lax.reduce_precision(router, 8, 7)
    low = router - high
    tail = jnp.concatenate([high, low], axis=1).astype(BF16)
    tail = jnp.pad(tail, ((0, 0), (0, 128 - tail.shape[1])))
    mine = jnp.concatenate([tokens, tail], axis=1)
    own_rows = lax.all_to_all(
        jnp.broadcast_to(mine[None], (NQ,) + mine.shape),
        "task",
        0,
        0,
        axis_index_groups=CHIPS,
    )
    other_rows = permute(own_rows, CORE)

    width_sum = ranks + feats
    payload = call(
        functools.partial(latent_kernel, width),
        sds((NQ, 2 * rows, width_sum)),
        own_rows,
        other_rows,
        lower_factor,
        low_other,
        scalars=s,
        grid=(1,),
        in_specs=[whole(own_rows), whole(other_rows), own_spec(lower_factor), whole(low_other)],
        out_specs=whole(sds((NQ, 2 * rows, width_sum))),
    )
    group = NQ * 2 * rows // tensor
    got = lax.all_to_all(payload.reshape(tensor, group, width_sum), "tensor", 0, 0)
    back = simple(
        functools.partial(mid_kernel, ranks), sds((tensor, group, width_sum)), got, scalars=s
    )
    got = lax.all_to_all(back, "tensor", 0, 0).reshape(NQ, 2 * rows, width_sum)

    block = 512
    m = NZ * 2 * rows
    tile = pl.BlockSpec((m, block), lambda i, s: (0, i))
    parts = call(
        functools.partial(main_kernel, ranks),
        [sds((m, hid), F32)] + [sds((m, hid))] * 3,
        got,
        gate_up_weight,
        w_other,
        upper_factor,
        u_other,
        scalars=s,
        grid=(pl.cdiv(hid, block),),
        in_specs=[
            whole(got),
            own_spec(gate_up_weight, block),
            pl.BlockSpec((w_other.shape[0], block), lambda i, s: (0, i)),
            own_spec(upper_factor, block),
            pl.BlockSpec((u_other.shape[0], block), lambda i, s: (0, i)),
        ],
        out_specs=[tile] * 4,
        scratch_shapes=[pltpu.VMEM((NQ * 2 * rows, width_sum), BF16)],
    )
    got = [permute(parts[d], TO_X[d]) for d in (2, 1, 3)]
    m = 2 * rows
    parts = simple(
        x_sum_kernel, [sds((m, hid), F32)] + [sds((m, hid))] * 3, parts[0], *got, scalars=s
    )
    got = [permute(parts[d], TO_Z[d]) for d in (2, 1, 3)]
    keep, send = simple(z_sum_kernel, [sds((rows, hid), F32)] * 2, parts[0], *got, scalars=s)
    hidden = simple(silu_kernel, sds((rows, hid)), keep, permute(send, CORE), scalars=s)

    got = {d: permute(hidden, TO_Z[d]) for d in (2, 1, 3)}
    hidden = jnp.concatenate([hidden, got[1], got[2], got[3]], axis=0)
    got = {d: permute(hidden, TO_X[d]) for d in (2, 1, 3)}
    first = c == 0
    cols = down_weight.shape[1]
    mixed = simple(
        down_kernel,
        sds((NQ, rows, 2 * cols)),
        hidden,
        got[1],
        got[2],
        got[3],
        down_weight,
        down_other,
        scalars=s,
    )
    got = lax.all_to_all(
        mixed.reshape(tensor, NQ // tensor, rows, 2 * cols), "tensor", 0, 0
    )
    keep, send = simple(
        out_sum_kernel, [sds((NQ // tensor, rows, cols), F32)] * 2, got, scalars=s
    )
    got = permute(send, CORE)
    out = jnp.stack([jnp.where(first, keep, got), jnp.where(first, got, keep)], axis=1)
    return out.reshape(NQ // tensor * NC * rows, cols)


def solution(mesh):
    in_specs = (
        P("task", "tensor"),
        P("task", None),
        P(None, "task", "tensor"),
        P("tensor", "task"),
        P(None, "tensor", "task"),
        P(None, "task", "tensor"),
    )
    out_specs = P("tensor", "task")
    return jax.shard_map(
        on_device, mesh=mesh, in_specs=in_specs, out_specs=out_specs, check_vma=False
    )
```

```python
import functools

import jax
import jax.numpy as jnp
from jax import lax
from jax.experimental import pallas as pl
from jax.experimental.pallas import tpu as pltpu
from jax.sharding import PartitionSpec as P

F32 = jnp.float32
BF16 = jnp.bfloat16
TASKS = 16
NX, NZ, NC = 4, 4, 2
NQ = NX * NZ
VMEM_BYTES = 48 * 1024 * 1024


def task_of(x, z, c):
    return (x * NZ + z) * NC + c


def task_perm(move):
    pairs = []
    for x in range(NX):
        for z in range(NZ):
            for c in range(NC):
                pairs.append((task_of(x, z, c), task_of(*move(x, z, c))))
    return pairs


CORE = task_perm(lambda x, z, c: (x, z, 1 - c))
TO_X = {d: task_perm(lambda x, z, c, d=d: ((x + d) % NX, z, c)) for d in (1, 2, 3)}
TO_Z = {d: task_perm(lambda x, z, c, d=d: (x, (z + d) % NZ, c)) for d in (1, 2, 3)}
CHIPS = [[task_of(x, z, c) for x in range(NX) for z in range(NZ)] for c in range(NC)]
FAR_FIRST = (2, 1, 3)


def sds(shape, dtype=BF16):
    return jax.ShapeDtypeStruct(shape, dtype)


def whole(a):
    return pl.BlockSpec(a.shape, lambda *_: (0,) * len(a.shape))


def call(kernel, out_shape, *args, scalars, grid=(1,), in_specs=None, out_specs=None, scratch=()):
    many = isinstance(out_shape, (list, tuple))
    if in_specs is None:
        in_specs = [whole(a) for a in args]
    if out_specs is None:
        out_specs = [whole(o) for o in out_shape] if many else whole(out_shape)
    return pl.pallas_call(
        kernel,
        out_shape=out_shape,
        grid_spec=pltpu.PrefetchScalarGridSpec(
            num_scalar_prefetch=1,
            grid=grid,
            in_specs=in_specs,
            out_specs=out_specs,
            scratch_shapes=list(scratch),
        ),
        compiler_params=pltpu.CompilerParams(vmem_limit_bytes=VMEM_BYTES),
    )(scalars, *args)


def rows_of(v):
    v = v.astype(F32)
    return v.reshape(v.shape[0] * v.shape[1], v.shape[2])


def pack_kernel(s, tokens, router, to_chips, to_tensor):
    high = router[...].astype(BF16)
    low = (router[...] - high.astype(F32)).astype(BF16)
    lane = lax.broadcasted_iota(jnp.int32, (TASKS, 128), 1)
    row = lax.broadcasted_iota(jnp.int32, (TASKS, 128), 0)
    tail = jnp.dot(high, (lane == row).astype(BF16), preferred_element_type=F32)
    tail += jnp.dot(low, (lane == row + TASKS).astype(BF16), preferred_element_type=F32)
    width = tokens.shape[1]
    for i in range(to_chips.shape[0]):
        to_chips[i, :, :width] = tokens[...]
        to_chips[i, :, width:] = tail.astype(BF16)
    for i in range(to_tensor.shape[0]):
        to_tensor[i] = tokens[...]


def latent_kernel(width, s, own, other, low_own, low_other, out):
    q = s[3]
    x = jnp.concatenate([rows_of(own[...]), rows_of(other[...])], axis=0)
    low = jnp.concatenate([low_own[0], low_other[...]], axis=1)
    lat = jnp.dot(x[:, :width].astype(BF16), low, preferred_element_type=F32)
    tail = x[:, width:]
    lane = lax.broadcasted_iota(jnp.int32, tail.shape, 1)
    weight = jnp.sum(
        jnp.where((lane == q) | (lane == TASKS + q), tail, 0.0), axis=1, keepdims=True
    )
    lat = (lat * weight).astype(BF16)
    for j in range(out.shape[0]):
        out[j] = lat


def gather_rows_kernel(s, lat, own, other, out):
    c = s[2]
    half = own.shape[2] // 2
    m = out.shape[0] // 2
    a = pl.multiple_of(c * half, half)
    b = pl.multiple_of((1 - c) * half, half)
    for k, ref in enumerate((own, other)):
        out[k * m : (k + 1) * m, :half] = rows_of(ref[:, :, pl.ds(a, half)]).astype(BF16)
        out[k * m : (k + 1) * m, half : 2 * half] = rows_of(ref[:, :, pl.ds(b, half)]).astype(
            BF16
        )
    total = lat[0].astype(F32)
    for j in range(1, lat.shape[0]):
        total += lat[j].astype(F32)
    out[:, 2 * half :] = total.astype(BF16)


def main_kernel(d, limit, s, rows, w_own, w_other, u_own, u_other, out):
    w = jnp.concatenate([w_own[0], w_other[...], u_own[0], u_other[...]], axis=1)
    p = lax.dot_general(w, rows[...], (((1,), (1,)), ((), ())), preferred_element_type=F32)
    start = (lax.rem(s[0] + d, NX) * 2 + pl.program_id(0)) * p.shape[0]
    at = start + lax.broadcasted_iota(jnp.int32, p.shape, 0)
    p = jnp.where(at < limit, p, 0.0)
    m = out.shape[1]
    out[0] = p[:m].astype(out.dtype)
    out[1] = p[m:].astype(out.dtype)


def x_sum_kernel(s, a0, a1, a2, a3, o0, o1, o2, o3):
    for i, o in enumerate((o0, o1, o2, o3)):
        k = lax.rem(s[1] + i, NZ)
        t = a0[k] + a1[k].astype(F32) + a2[k].astype(F32) + a3[k].astype(F32)
        o[...] = t.astype(o.dtype)


def z_sum_kernel(s, a0, a1, a2, a3, keep, send):
    t = a0[...] + a1[...].astype(F32) + a2[...].astype(F32) + a3[...].astype(F32)
    m = keep.shape[1]
    keep[...] = t[:, :m]
    send[...] = t[:, m:]


def silu_kernel(s, keep, got, out):
    first = s[2] == 0
    gate = jnp.where(first, keep[...], got[...])
    up = jnp.where(first, got[...], keep[...])
    out[...] = (gate / (1.0 + jnp.exp(-gate)) * up).astype(BF16)


def split_kernel(limit, s, w0, w1, w2, w3, *outs):
    for d, (w, o) in enumerate(zip((w0, w1, w2, w3), outs)):
        at = lax.rem(s[0] + d, NX) * w.shape[0] + lax.broadcasted_iota(jnp.int32, w.shape, 0)
        o[...] = jnp.where(at < limit, w[...].astype(F32), 0.0).astype(BF16)


def down_kernel(s, h0, h1, h2, h3, *rest):
    weights, (out, held) = rest[:-2], rest[-2:]
    m = h0.shape[0]
    for d, h in enumerate((h0, h1, h2, h3)):
        k = lax.rem(s[1] - d + NZ, NZ)
        held[pl.ds(pl.multiple_of(m * k, 8), m)] = h[...].astype(F32)
    h = held[...].T.astype(BF16)
    cols = weights[0].shape[1]
    for i, w in enumerate(weights):
        p = jnp.dot(h, w[...], preferred_element_type=F32).astype(BF16)
        out[:, :, i * cols : (i + 1) * cols] = p.reshape(out.shape[0], out.shape[1], cols)


def tensor_sum_kernel(s, got, o0, o1, o2, o3):
    t = got[0].astype(F32)
    for j in range(1, got.shape[0]):
        t += got[j].astype(F32)
    cols = o0.shape[1] // 2
    for d, o in enumerate((o0, o1, o2, o3)):
        o[:, :cols] = t[:, d * cols : (d + 1) * cols].astype(o.dtype)
        o[:, cols:] = t[:, (NX + d) * cols : (NX + d + 1) * cols].astype(o.dtype)


def out_sum_kernel(s, a0, a1, a2, a3, keep, send):
    t = a0[...] + a1[...].astype(F32) + a2[...].astype(F32) + a3[...].astype(F32)
    cols = keep.shape[1]
    keep[...] = t[:, :cols]
    send[...] = t[:, cols:]


def place_kernel(s, keep, got, out):
    first = s[2] == 0
    a = jnp.where(first, keep[...], got[...])
    b = jnp.where(first, got[...], keep[...])
    for i in range(out.shape[0] // 16):
        out[16 * i : 16 * i + 8] = a[8 * i : 8 * i + 8]
        out[16 * i + 8 : 16 * i + 16] = b[8 * i : 8 * i + 8]


def on_device(tokens, router, gate_up_weight, down_weight, lower_factor, upper_factor):
    t = lax.axis_index("task").astype(jnp.int32)
    c = lax.rem(t, NC)
    q = t // NC
    x, z = q // NZ, lax.rem(q, NZ)
    s = jnp.stack([x, z, c, q])
    tensor = lax.axis_size("tensor")
    run = functools.partial(call, scalars=s)

    def permute(a, perm):
        return lax.ppermute(a, "task", perm)

    def chips(a):
        return lax.all_to_all(a, "task", 0, 0, axis_index_groups=CHIPS)

    def across(a):
        return lax.all_to_all(a, "tensor", 0, 0)

    def other(a):
        return lax.dynamic_index_in_dim(a, 1 - c, 0, keepdims=False)

    rows, width = tokens.shape
    ranks = 2 * lower_factor.shape[2]
    feats = 2 * gate_up_weight.shape[1]
    hid = gate_up_weight.shape[2]
    count = NQ * NC * rows
    weight = jnp.swapaxes(gate_up_weight, 1, 2)
    upper = jnp.swapaxes(upper_factor, 1, 2)
    zb = -(-hid // (NX * NZ * 8)) * 8
    xb = NZ * zb

    low_other = permute(other(lower_factor), CORE)
    w_other = permute(other(weight), CORE)
    u_other = permute(other(upper), CORE)

    to_chips, to_tensor = run(
        pack_kernel,
        [sds((NQ, rows, width + 128)), sds((tensor, rows, width))],
        tokens,
        router,
    )
    own_rows = chips(to_chips)
    full = across(to_tensor)
    other_rows = permute(own_rows, CORE)
    full = full.reshape(tensor, rows, width // feats, feats).transpose(0, 2, 1, 3)
    own_cols = chips(full.reshape(NQ, rows, feats))
    other_cols = permute(own_cols, CORE)

    lat = run(
        functools.partial(latent_kernel, width),
        sds((tensor, count, ranks)),
        own_rows,
        other_rows,
        lower_factor,
        low_other,
        in_specs=[
            whole(own_rows),
            whole(other_rows),
            pl.BlockSpec((1,) + lower_factor.shape[1:], lambda i, s: (s[2], 0, 0)),
            whole(low_other),
        ],
    )
    lat = across(lat)

    pieces = run(
        functools.partial(split_kernel, hid),
        [sds((xb, down_weight.shape[1]))] * NX,
        *[down_weight] * NX,
        in_specs=[
            pl.BlockSpec(
                (xb, down_weight.shape[1]), lambda i, s, d=d: (lax.rem(s[0] + d, NX), 0)
            )
            for d in range(NX)
        ],
    )
    got = {d: permute(pieces[d], TO_X[d]) for d in FAR_FIRST}
    down_own = [pieces[0], got[1], got[2], got[3]]
    down_other = [permute(a, CORE) for a in down_own]

    cat = run(gather_rows_kernel, sds((count, feats + ranks)), lat, own_cols, other_cols)
    block = 2 * zb

    def main(d, dtype):
        def at(i, s):
            return lax.rem(s[0] + d, NX) * 2 + i

        def own_spec(a):
            return pl.BlockSpec((1, block, a.shape[2]), lambda i, s: (s[2], at(i, s), 0))

        def spec(a):
            return pl.BlockSpec((block, a.shape[1]), lambda i, s: (at(i, s), 0))

        return run(
            functools.partial(main_kernel, d, hid),
            sds((NZ, zb, count), dtype),
            cat,
            weight,
            w_other,
            upper,
            u_other,
            grid=(2,),
            in_specs=[whole(cat), own_spec(weight), spec(w_other), own_spec(upper), spec(u_other)],
            out_specs=pl.BlockSpec((2, zb, count), lambda i, s: (i, 0, 0)),
        )

    got = {d: permute(main(d, BF16), TO_X[d]) for d in FAR_FIRST}
    parts = run(
        x_sum_kernel,
        [sds((zb, count), F32)] + [sds((zb, count))] * 3,
        main(0, F32),
        got[1],
        got[2],
        got[3],
    )
    got = {d: permute(parts[d], TO_Z[d]) for d in FAR_FIRST}
    keep, send = run(
        z_sum_kernel, [sds((zb, count // 2), F32)] * 2, parts[0], got[1], got[2], got[3]
    )
    hidden = run(silu_kernel, sds((zb, count // 2)), keep, permute(send, CORE))

    got = {d: permute(hidden, TO_Z[d]) for d in FAR_FIRST}
    cols = down_weight.shape[1]
    out_rows = count // 2 // tensor
    mixed = run(
        down_kernel,
        sds((tensor, out_rows, 2 * NX * cols)),
        hidden,
        got[1],
        got[2],
        got[3],
        *down_own,
        *down_other,
        scratch=[pltpu.VMEM((xb, count // 2), F32)],
    )
    parts = run(
        tensor_sum_kernel,
        [sds((out_rows, 2 * cols), F32)] + [sds((out_rows, 2 * cols))] * 3,
        across(mixed),
    )
    got = {d: permute(parts[d], TO_X[NX - d]) for d in FAR_FIRST}
    keep, send = run(
        out_sum_kernel, [sds((out_rows, cols), F32)] * 2, parts[0], got[1], got[2], got[3]
    )
    return run(place_kernel, sds((2 * out_rows, cols), F32), keep, permute(send, CORE))


def solution(mesh):
    in_specs = (
        P("task", "tensor"),
        P("task", None),
        P(None, "task", "tensor"),
        P("tensor", "task"),
        P(None, "tensor", "task"),
        P(None, "task", "tensor"),
    )
    out_specs = P("tensor", "task")
    return jax.shard_map(
        on_device, mesh=mesh, in_specs=in_specs, out_specs=out_specs, check_vma=False
    )
```

```python
import functools

import jax
import jax.numpy as jnp
from jax import lax
from jax.experimental import pallas as pl
from jax.experimental.pallas import tpu as pltpu
from jax.sharding import PartitionSpec as P

F32 = jnp.float32
BF16 = jnp.bfloat16
TASKS = 16
NX, NZ, NC = 4, 4, 2
NQ = NX * NZ
VMEM_BYTES = 48 * 1024 * 1024


def task_of(x, z, c):
    return (x * NZ + z) * NC + c


def task_perm(move):
    pairs = []
    for x in range(NX):
        for z in range(NZ):
            for c in range(NC):
                pairs.append((task_of(x, z, c), task_of(*move(x, z, c))))
    return pairs


CORE = task_perm(lambda x, z, c: (x, z, 1 - c))
TO_X = {d: task_perm(lambda x, z, c, d=d: ((x + d) % NX, z, c)) for d in (1, 2, 3)}
TO_Z = {d: task_perm(lambda x, z, c, d=d: (x, (z + d) % NZ, c)) for d in (1, 2, 3)}
CHIPS = [[task_of(x, z, c) for x in range(NX) for z in range(NZ)] for c in range(NC)]
FAR_FIRST = (2, 1, 3)


def sds(shape, dtype=BF16):
    return jax.ShapeDtypeStruct(shape, dtype)


def whole(a):
    return pl.BlockSpec(a.shape, lambda *_: (0,) * len(a.shape))


def call(kernel, out_shape, *args, scalars, grid=(1,), in_specs=None, out_specs=None, scratch=()):
    many = isinstance(out_shape, (list, tuple))
    if in_specs is None:
        in_specs = [whole(a) for a in args]
    if out_specs is None:
        out_specs = [whole(o) for o in out_shape] if many else whole(out_shape)
    return pl.pallas_call(
        kernel,
        out_shape=out_shape,
        grid_spec=pltpu.PrefetchScalarGridSpec(
            num_scalar_prefetch=1,
            grid=grid,
            in_specs=in_specs,
            out_specs=out_specs,
            scratch_shapes=list(scratch),
        ),
        compiler_params=pltpu.CompilerParams(vmem_limit_bytes=VMEM_BYTES),
    )(scalars, *args)


def rows_of(v):
    v = v.astype(F32)
    return v.reshape(v.shape[0] * v.shape[1], v.shape[2])


def pack_kernel(s, tokens, router, out):
    high = router[...].astype(BF16)
    low = (router[...] - high.astype(F32)).astype(BF16)
    lane = lax.broadcasted_iota(jnp.int32, (TASKS, 128), 1)
    row = lax.broadcasted_iota(jnp.int32, (TASKS, 128), 0)
    tail = jnp.dot(high, (lane == row).astype(BF16), preferred_element_type=F32)
    tail += jnp.dot(low, (lane == row + TASKS).astype(BF16), preferred_element_type=F32)
    width = tokens.shape[1]
    for i in range(out.shape[0]):
        out[i, :, :width] = tokens[...]
        out[i, :, width:] = tail.astype(BF16)


def latent_kernel(width, s, own, other, low_own, low_other, out):
    q = s[3]
    x = jnp.concatenate([rows_of(own[...]), rows_of(other[...])], axis=0)
    low = jnp.concatenate([low_own[0], low_other[...]], axis=1)
    lat = jnp.dot(x[:, :width].astype(BF16), low, preferred_element_type=F32)
    tail = x[:, width:]
    lane = lax.broadcasted_iota(jnp.int32, tail.shape, 1)
    weight = jnp.sum(
        jnp.where((lane == q) | (lane == TASKS + q), tail, 0.0), axis=1, keepdims=True
    )
    ranks = lat.shape[1]
    out[:, :ranks] = (lat * weight).astype(BF16)
    feats = out.shape[1] - ranks
    start = pl.multiple_of(lax.rem(q, 2) * feats, feats)
    m = out.shape[0] // 2
    for k, ref in enumerate((own, other)):
        part = rows_of(ref[:, :, pl.ds(start, feats)])
        out[k * m : (k + 1) * m, ranks:] = part.astype(BF16)


def mid_kernel(ranks, s, got, out):
    c = s[2]
    total = got[0, :, :ranks].astype(F32)
    for j in range(1, got.shape[0]):
        total += got[j, :, :ranks].astype(F32)
    half = (got.shape[2] - ranks) // 2
    own = got[s[3] // 2, :, pl.ds(pl.multiple_of(ranks + c * half, half), half)]
    other = got[s[3] // 2, :, pl.ds(pl.multiple_of(ranks + (1 - c) * half, half), half)]
    for j in range(out.shape[0]):
        out[j, :, :half] = own
        out[j, :, half : 2 * half] = other
        out[j, :, 2 * half :] = total.astype(BF16)


def main_kernel(d, limit, s, rows, w_own, w_other, u_own, u_other, out_a, out_b):
    w = jnp.concatenate([w_own[0], w_other[...], u_own[0], u_other[...]], axis=1)
    p = lax.dot_general(w, rows[...], (((1,), (1,)), ((), ())), preferred_element_type=F32)
    i = pl.program_id(0)
    start = (lax.rem(s[0] + d, NX) * 2 + i) * p.shape[0]
    at = start + lax.broadcasted_iota(jnp.int32, p.shape, 0)
    p = jnp.where(at < limit, p, 0.0)
    m = out_a.shape[1]

    @pl.when(i == 0)
    def _():
        out_a[0] = p[:m].astype(out_a.dtype)
        out_a[1] = p[m:].astype(out_a.dtype)

    @pl.when(i == 1)
    def _():
        out_b[0] = p[:m].astype(out_b.dtype)
        out_b[1] = p[m:].astype(out_b.dtype)


def pass_kernel(s, a, got_a, b, got_b, out_a, out_b):
    out_a[...] = (a[...] + got_a[...].astype(F32)).astype(BF16)
    out_b[...] = (b[...] + got_b[...].astype(F32)).astype(BF16)


def x_sum_kernel(s, a0, a1, a2, b0, b1, b2, o0, o1, o2, o3, held):
    for k in range(2):
        held[k] = a0[k] + a1[k].astype(F32) + a2[k].astype(F32)
        held[2 + k] = b0[k] + b1[k].astype(F32) + b2[k].astype(F32)
    for i, o in enumerate((o0, o1, o2, o3)):
        o[...] = held[lax.rem(s[1] + i, NZ)].astype(o.dtype)


def z_sum_kernel(s, a0, a1, a2, a3, keep, send):
    t = a0[...] + a1[...].astype(F32) + a2[...].astype(F32) + a3[...].astype(F32)
    m = keep.shape[1]
    keep[...] = t[:, :m]
    send[...] = t[:, m:]


def silu_kernel(s, keep, got, out):
    first = s[2] == 0
    gate = jnp.where(first, keep[...], got[...])
    up = jnp.where(first, got[...], keep[...])
    out[...] = (gate / (1.0 + jnp.exp(-gate)) * up).astype(BF16)


def stack_kernel(s, h0, h1, h2, h3, out):
    for d, h in enumerate((h0, h1, h2, h3)):
        out[lax.rem(s[1] - d + NZ, NZ)] = h[...]


def down_kernel(s, h0, h1, h2, h3, w_own, w_other, out, held):
    n, m = h0.shape[:2]
    for d, h in enumerate((h0, h1, h2, h3)):
        start = lax.rem(s[0] - d + NX, NX) * (n * m)
        for k in range(n):
            held[pl.ds(pl.multiple_of(start + k * m, 8), m)] = h[k].astype(F32)
    h = held[...].T.astype(BF16)
    deep, cols = w_own.shape
    for i, w in enumerate((w_own, w_other)):
        p = jnp.dot(h[:, :deep], w[...], preferred_element_type=F32).astype(BF16)
        out[:, :, i * cols : (i + 1) * cols] = p.reshape(out.shape[0], out.shape[1], cols)


def tensor_sum_kernel(s, got, keep, send):
    t = got[0].astype(F32)
    for j in range(1, got.shape[0]):
        t += got[j].astype(F32)
    cols = keep.shape[1]
    keep[...] = t[:, :cols]
    send[...] = t[:, cols:]


def place_kernel(s, keep, got, out):
    first = s[2] == 0
    a = jnp.where(first, keep[...], got[...])
    b = jnp.where(first, got[...], keep[...])
    for i in range(out.shape[0] // 16):
        out[16 * i : 16 * i + 8] = a[8 * i : 8 * i + 8]
        out[16 * i + 8 : 16 * i + 16] = b[8 * i : 8 * i + 8]


def on_device(tokens, router, gate_up_weight, down_weight, lower_factor, upper_factor):
    t = lax.axis_index("task").astype(jnp.int32)
    c = lax.rem(t, NC)
    q = t // NC
    x, z = q // NZ, lax.rem(q, NZ)
    s = jnp.stack([x, z, c, q])
    tensor = lax.axis_size("tensor")
    run = functools.partial(call, scalars=s)

    def permute(a, perm):
        return lax.ppermute(a, "task", perm)

    def across(a):
        return lax.all_to_all(a, "tensor", 0, 0)

    def other(a):
        return lax.dynamic_index_in_dim(a, 1 - c, 0, keepdims=False)

    rows, width = tokens.shape
    ranks = 2 * lower_factor.shape[2]
    feats = 2 * gate_up_weight.shape[1]
    hid = gate_up_weight.shape[2]
    count = NQ * NC * rows
    weight = jnp.swapaxes(gate_up_weight, 1, 2)
    upper = jnp.swapaxes(upper_factor, 1, 2)
    zb = -(-hid // (NX * NZ * 8)) * 8
    xb = NZ * zb

    low_other = permute(other(lower_factor), CORE)
    w_other = permute(other(weight), CORE)
    u_other = permute(other(upper), CORE)
    down_other = permute(down_weight, CORE)

    packed = run(pack_kernel, sds((NQ, rows, width + 128)), tokens, router)
    own_rows = lax.all_to_all(packed, "task", 0, 0, axis_index_groups=CHIPS)
    other_rows = permute(own_rows, CORE)
    lat = run(
        functools.partial(latent_kernel, width),
        sds((count, ranks + feats)),
        own_rows,
        other_rows,
        lower_factor,
        low_other,
        in_specs=[
            whole(own_rows),
            whole(other_rows),
            pl.BlockSpec((1,) + lower_factor.shape[1:], lambda i, s: (s[2], 0, 0)),
            whole(low_other),
        ],
    )
    got = across(lat.reshape(tensor, count // tensor, ranks + feats))
    mid = run(functools.partial(mid_kernel, ranks), sds(got.shape), got)
    cat = across(mid).reshape(count, feats + ranks)

    block = 2 * zb

    def main(d, dtype_a, dtype_b):
        def at(i, s):
            return lax.rem(s[0] + d, NX) * 2 + i

        def own_spec(a):
            return pl.BlockSpec((1, block, a.shape[2]), lambda i, s: (s[2], at(i, s), 0))

        def spec(a):
            return pl.BlockSpec((block, a.shape[1]), lambda i, s: (at(i, s), 0))

        return run(
            functools.partial(main_kernel, d, hid),
            [sds((2, zb, count), dtype_a), sds((2, zb, count), dtype_b)],
            cat,
            weight,
            w_other,
            upper,
            u_other,
            grid=(2,),
            in_specs=[whole(cat), own_spec(weight), spec(w_other), own_spec(upper), spec(u_other)],
        )

    far_a, far_b = main(2, BF16, BF16)
    far_a = permute(far_a, TO_X[1])
    far_b = permute(far_b, TO_X[3])
    up_a, up_b = main(1, F32, BF16)
    down_a, down_b = main(3, BF16, F32)
    up_b = permute(up_b, TO_X[1])
    down_a = permute(down_a, TO_X[3])
    up_a, down_b = run(pass_kernel, [sds(far_a.shape)] * 2, up_a, far_a, down_b, far_b)
    up_a = permute(up_a, TO_X[1])
    down_b = permute(down_b, TO_X[3])
    own_a, own_b = main(0, F32, F32)
    parts = run(
        x_sum_kernel,
        [sds((zb, count), F32)] + [sds((zb, count))] * 3,
        own_a,
        down_a,
        up_a,
        own_b,
        up_b,
        down_b,
        scratch=[pltpu.VMEM((NZ, zb, count), F32)],
    )
    got = {d: permute(parts[d], TO_Z[d]) for d in FAR_FIRST}
    keep, send = run(
        z_sum_kernel, [sds((zb, count // 2), F32)] * 2, parts[0], got[1], got[2], got[3]
    )
    hidden = run(silu_kernel, sds((zb, count // 2)), keep, permute(send, CORE))

    got = {d: permute(hidden, TO_Z[d]) for d in FAR_FIRST}
    hidden = run(stack_kernel, sds((NZ, zb, count // 2)), hidden, got[1], got[2], got[3])
    got = {d: permute(hidden, TO_X[d]) for d in FAR_FIRST}
    cols = down_weight.shape[1]
    out_rows = count // 2 // tensor
    mixed = run(
        down_kernel,
        sds((tensor, out_rows, 2 * cols)),
        hidden,
        got[1],
        got[2],
        got[3],
        down_weight,
        down_other,
        scratch=[pltpu.VMEM((NX * xb, count // 2), F32)],
    )
    keep, send = run(tensor_sum_kernel, [sds((out_rows, cols), F32)] * 2, across(mixed))
    return run(place_kernel, sds((2 * out_rows, cols), F32), keep, permute(send, CORE))


def solution(mesh):
    in_specs = (
        P("task", "tensor"),
        P("task", None),
        P(None, "task", "tensor"),
        P("tensor", "task"),
        P(None, "tensor", "task"),
        P(None, "task", "tensor"),
    )
    out_specs = P("tensor", "task")
    return jax.shard_map(
        on_device, mesh=mesh, in_specs=in_specs, out_specs=out_specs, check_vma=False
    )
```

```python
import functools

import jax
import jax.numpy as jnp
from jax import lax
from jax.experimental import pallas as pl
from jax.experimental.pallas import tpu as pltpu
from jax.sharding import PartitionSpec as P

F32 = jnp.float32
BF16 = jnp.bfloat16
TASKS = 16
NX, NZ, NC = 4, 4, 2
NQ = NX * NZ
VMEM_BYTES = 48 * 1024 * 1024
INSIDE_BYTES = 24 * 1024 * 1024


def task_of(x, z, c):
    return (x * NZ + z) * NC + c


def task_perm(move):
    pairs = []
    for x in range(NX):
        for z in range(NZ):
            for c in range(NC):
                pairs.append((task_of(x, z, c), task_of(*move(x, z, c))))
    return pairs


CORE = task_perm(lambda x, z, c: (x, z, 1 - c))
TO_X = {d: task_perm(lambda x, z, c, d=d: ((x + d) % NX, z, c)) for d in (1, 2, 3)}
TO_Z = {d: task_perm(lambda x, z, c, d=d: (x, (z + d) % NZ, c)) for d in (1, 2, 3)}
CHIPS = [[task_of(x, z, c) for x in range(NX) for z in range(NZ)] for c in range(NC)]
FAR_FIRST = (2, 1, 3)


def sds(shape, dtype=BF16):
    return jax.ShapeDtypeStruct(shape, dtype)


def whole(a):
    return pl.BlockSpec(a.shape, lambda *_: (0,) * len(a.shape))


def call(kernel, out_shape, *args, scalars, grid=(1,), in_specs=None, out_specs=None, scratch=()):
    many = isinstance(out_shape, (list, tuple))
    if in_specs is None:
        in_specs = [whole(a) for a in args]
    if out_specs is None:
        out_specs = [whole(o) for o in out_shape] if many else whole(out_shape)
    return pl.pallas_call(
        kernel,
        out_shape=out_shape,
        grid_spec=pltpu.PrefetchScalarGridSpec(
            num_scalar_prefetch=1,
            grid=grid,
            in_specs=in_specs,
            out_specs=out_specs,
            scratch_shapes=list(scratch),
        ),
        compiler_params=pltpu.CompilerParams(vmem_limit_bytes=VMEM_BYTES),
    )(scalars, *args)


def call_inside(kernel, out_shape, *args, scalars, hbm=0, scratch=()):
    inside = pl.BlockSpec(memory_space=pltpu.VMEM)
    specs = [pl.BlockSpec(memory_space=pltpu.HBM)] * hbm + [inside] * (len(args) - hbm)
    many = isinstance(out_shape, (list, tuple))
    return pl.pallas_call(
        kernel,
        out_shape=out_shape,
        in_specs=[pl.BlockSpec(memory_space=pltpu.SMEM)] + specs,
        out_specs=[inside] * len(out_shape) if many else inside,
        scratch_shapes=list(scratch),
        compiler_params=pltpu.CompilerParams(vmem_limit_bytes=INSIDE_BYTES),
    )(scalars, *args)


def rows_of(v):
    v = v.astype(F32)
    return v.reshape(v.shape[0] * v.shape[1], v.shape[2])


def latent_kernel(width, s, own, other, low_own, low_other, out):
    q = s[3]
    x = jnp.concatenate([rows_of(own[...]), rows_of(other[...])], axis=0)
    low = jnp.concatenate([low_own[0], low_other[...]], axis=1)
    lat = jnp.dot(x[:, :width].astype(BF16), low, preferred_element_type=F32)
    tail = x[:, width:]
    lane = lax.broadcasted_iota(jnp.int32, tail.shape, 1)
    weight = jnp.sum(
        jnp.where((lane == q) | (lane == TASKS + q), tail, 0.0), axis=1, keepdims=True
    )
    ranks = lat.shape[1]
    out[:, :ranks] = (lat * weight).astype(BF16)
    feats = out.shape[1] - ranks
    start = pl.multiple_of(lax.rem(q, 2) * feats, feats)
    m = out.shape[0] // 2
    for k, ref in enumerate((own, other)):
        part = rows_of(ref[:, :, pl.ds(start, feats)])
        out[k * m : (k + 1) * m, ranks:] = part.astype(BF16)


def mid_kernel(ranks, s, got, out):
    c = s[2]
    total = got[0, :, :ranks].astype(F32)
    for j in range(1, got.shape[0]):
        total += got[j, :, :ranks].astype(F32)
    half = (got.shape[2] - ranks) // 2
    own = got[s[3] // 2, :, pl.ds(pl.multiple_of(ranks + c * half, half), half)]
    other = got[s[3] // 2, :, pl.ds(pl.multiple_of(ranks + (1 - c) * half, half), half)]
    for j in range(out.shape[0]):
        out[j, :, :half] = own
        out[j, :, half : 2 * half] = other
        out[j, :, 2 * half :] = total.astype(BF16)


def pick(i, values):
    v = values[0]
    for k in range(1, len(values)):
        v = jnp.where(i == k, values[k], v)
    return v


def main_kernel(limit, halves, s, rows, w_own, w_other, u_own, u_other, *outs):
    i = pl.program_id(0)
    w = jnp.concatenate([w_own[0], w_other[...], u_own[0], u_other[...]], axis=1)
    p = lax.dot_general(w, rows[...], (((1,), (1,)), ((), ())), preferred_element_type=F32)
    n = p.shape[0]
    at = half_block(halves, i, s) * n + lax.broadcasted_iota(jnp.int32, p.shape, 0)
    p = jnp.where(at < limit, p, 0.0)
    for k, out in enumerate(outs):

        @pl.when(i == k)
        def _():
            out[0] = p[: n // 2].astype(out.dtype)
            out[1] = p[n // 2 :].astype(out.dtype)


def half_block(halves, i, s):
    d = pick(i, [d for d, _ in halves])
    return lax.rem(s[0] + d, NX) * 2 + pick(i, [h for _, h in halves])


def pass_kernel(s, a, got_a, b, got_b, out_a, out_b):
    out_a[...] = (a[...] + got_a[...].astype(F32)).astype(BF16)
    out_b[...] = (b[...] + got_b[...].astype(F32)).astype(BF16)


def x_sum_kernel(s, a0, a1, a2, b0, b1, b2, o0, o1, o2, o3, held):
    for k in range(2):
        held[k] = a0[k] + a1[k].astype(F32) + a2[k].astype(F32)
        held[2 + k] = b0[k] + b1[k].astype(F32) + b2[k].astype(F32)
    for i, o in enumerate((o0, o1, o2, o3)):
        o[...] = held[lax.rem(s[1] + i, NZ)].astype(o.dtype)


def z_sum_kernel(s, a0, a1, a2, a3, keep, send):
    t = a0[...] + a1[...].astype(F32) + a2[...].astype(F32) + a3[...].astype(F32)
    m = keep.shape[1]
    keep[...] = t[:, :m]
    send[...] = t[:, m:]


def silu_kernel(s, keep, got, out):
    first = s[2] == 0
    gate = jnp.where(first, keep[...], got[...])
    up = jnp.where(first, got[...], keep[...])
    out[...] = (gate / (1.0 + jnp.exp(-gate)) * up).astype(BF16)


def stack_kernel(s, h0, h1, h2, h3, out):
    for d, h in enumerate((h0, h1, h2, h3)):
        out[lax.rem(s[1] - d + NZ, NZ)] = h[...]


def down_rows(d, s, h, held, deep_all):
    n, m = h.shape[:2]
    deep = n * m
    held[:16] = jnp.zeros((16, held.shape[1]), F32)
    for k in range(n):
        held[16 + k * m : 16 + (k + 1) * m] = h[k].astype(F32)
    at = lax.rem(s[0] - d + NX, NX)
    shift = jnp.where(at == NX - 1, NX * deep - deep_all, 0)
    t = held[pl.ds(pl.multiple_of(16 - shift, 8), deep)].T.astype(BF16)
    return t, pl.ds(pl.multiple_of(at * deep - shift, 16), deep)


def down_own_kernel(s, w_own, w_other, h, w, out, held, sems):
    cols = w_own.shape[1]
    copies = [
        pltpu.make_async_copy(ref, w.at[:, pl.ds(i * cols, cols)], sems.at[i])
        for i, ref in enumerate((w_own, w_other))
    ]
    for copy in copies:
        copy.start()
    t, at = down_rows(0, s, h, held, w.shape[0])
    for copy in copies:
        copy.wait()
    out[...] = jnp.dot(t, w[at], preferred_element_type=F32)


def down_kernel(s, acc, h1, h2, h3, w, out, held):
    p = acc[...]
    for d, h in enumerate((h1, h2, h3), 1):
        t, at = down_rows(d, s, h, held.at[d - 1], w.shape[0])
        p += jnp.dot(t, w[at], preferred_element_type=F32)
    out[...] = p.astype(BF16).reshape(out.shape)


def tensor_sum_kernel(s, got, keep, send):
    t = got[0].astype(F32)
    for j in range(1, got.shape[0]):
        t += got[j].astype(F32)
    cols = keep.shape[1]
    keep[...] = t[:, :cols]
    send[...] = t[:, cols:]


def place_kernel(s, keep, got, out):
    first = s[2] == 0
    a = jnp.where(first, keep[...], got[...])
    b = jnp.where(first, got[...], keep[...])
    for i in range(out.shape[0] // 16):
        out[16 * i : 16 * i + 8] = a[8 * i : 8 * i + 8]
        out[16 * i + 8 : 16 * i + 16] = b[8 * i : 8 * i + 8]


def on_device(tokens, router, gate_up_weight, down_weight, lower_factor, upper_factor):
    t = lax.axis_index("task").astype(jnp.int32)
    c = lax.rem(t, NC)
    q = t // NC
    x, z = q // NZ, lax.rem(q, NZ)
    s = jnp.stack([x, z, c, q])
    tensor = lax.axis_size("tensor")
    run = functools.partial(call, scalars=s)

    def permute(a, perm):
        return lax.ppermute(a, "task", perm)

    def across(a):
        return lax.all_to_all(a, "tensor", 0, 0)

    def other(a):
        return lax.dynamic_index_in_dim(a, 1 - c, 0, keepdims=False)

    rows, width = tokens.shape
    ranks = 2 * lower_factor.shape[2]
    feats = 2 * gate_up_weight.shape[1]
    hid = gate_up_weight.shape[2]
    count = NQ * NC * rows
    weight = jnp.swapaxes(gate_up_weight, 1, 2)
    upper = jnp.swapaxes(upper_factor, 1, 2)
    zb = -(-hid // (NX * NZ * 8)) * 8
    xb = NZ * zb

    low_other = permute(other(lower_factor), CORE)
    w_other = permute(other(weight), CORE)
    u_other = permute(other(upper), CORE)
    down_other = permute(down_weight, CORE)

    high = lax.reduce_precision(router, 8, 7)
    fill = jnp.zeros((rows, 128 - 2 * TASKS), BF16)
    packed = jnp.concatenate(
        [tokens, high.astype(BF16), (router - high).astype(BF16), fill], axis=1
    )
    packed = jnp.broadcast_to(packed[None], (NQ,) + packed.shape)
    own_rows = lax.all_to_all(packed, "task", 0, 0, axis_index_groups=CHIPS)
    other_rows = permute(own_rows, CORE)
    lat = run(
        functools.partial(latent_kernel, width),
        sds((count, ranks + feats)),
        own_rows,
        other_rows,
        lower_factor,
        low_other,
        in_specs=[
            whole(own_rows),
            whole(other_rows),
            pl.BlockSpec((1,) + lower_factor.shape[1:], lambda i, s: (s[2], 0, 0)),
            whole(low_other),
        ],
    )
    got = across(lat.reshape(tensor, count // tensor, ranks + feats))
    mid = run(functools.partial(mid_kernel, ranks), sds(got.shape), got)
    cat = across(mid).reshape(count, feats + ranks)

    inside = functools.partial(call_inside, scalars=s)
    def main(halves, dtype):
        def own_spec(a):
            return pl.BlockSpec(
                (1, xb // 2, a.shape[2]), lambda i, s: (s[2], half_block(halves, i, s), 0)
            )

        def spec(a):
            return pl.BlockSpec((xb // 2, a.shape[1]), lambda i, s: (half_block(halves, i, s), 0))

        return run(
            functools.partial(main_kernel, hid, halves),
            [sds((2, zb, count), dtype)] * len(halves),
            cat,
            weight,
            w_other,
            upper,
            u_other,
            grid=(len(halves),),
            in_specs=[whole(cat), own_spec(weight), spec(w_other), own_spec(upper), spec(u_other)],
        )

    far_a, far_b = main(((2, 0), (2, 1)), BF16)
    far_a = permute(far_a, TO_X[1])
    far_b = permute(far_b, TO_X[3])
    up_b, down_a = main(((1, 1), (3, 0)), BF16)
    up_b = permute(up_b, TO_X[1])
    down_a = permute(down_a, TO_X[3])
    up_a, down_b, own_a, own_b = main(((1, 0), (3, 1), (0, 0), (0, 1)), F32)
    up_a, down_b = run(pass_kernel, [sds(far_a.shape)] * 2, up_a, far_a, down_b, far_b)
    up_a = permute(up_a, TO_X[1])
    down_b = permute(down_b, TO_X[3])
    parts = run(
        x_sum_kernel,
        [sds((zb, count), F32)] + [sds((zb, count))] * 3,
        own_a,
        down_a,
        up_a,
        own_b,
        up_b,
        down_b,
        scratch=[pltpu.VMEM((NZ, zb, count), F32)],
    )
    got = {d: permute(parts[d], TO_Z[d]) for d in FAR_FIRST}
    keep, send = run(
        z_sum_kernel, [sds((zb, count // 2), F32)] * 2, parts[0], got[1], got[2], got[3]
    )
    hidden = run(silu_kernel, sds((zb, count // 2)), keep, permute(send, CORE))

    got = {d: permute(hidden, TO_Z[d]) for d in FAR_FIRST}
    hidden = run(stack_kernel, sds((NZ, zb, count // 2)), hidden, got[1], got[2], got[3])
    got = {d: permute(hidden, TO_X[d]) for d in FAR_FIRST}
    cols = down_weight.shape[1]
    out_rows = count // 2 // tensor
    half = count // 2
    down, mixed = inside(
        down_own_kernel,
        [sds((hid, 2 * cols)), sds((half, 2 * cols), F32)],
        down_weight,
        down_other,
        hidden,
        hbm=2,
        scratch=[pltpu.VMEM((xb + 16, half), F32), pltpu.SemaphoreType.DMA((2,))],
    )
    mixed = inside(
        down_kernel,
        sds((tensor, out_rows, 2 * cols)),
        mixed,
        got[1],
        got[2],
        got[3],
        down,
        scratch=[pltpu.VMEM((3, xb + 16, half), F32)],
    )
    keep, send = run(tensor_sum_kernel, [sds((out_rows, cols), F32)] * 2, across(mixed))
    return run(place_kernel, sds((2 * out_rows, cols), F32), keep, permute(send, CORE))


def solution(mesh):
    in_specs = (
        P("task", "tensor"),
        P("task", None),
        P(None, "task", "tensor"),
        P("tensor", "task"),
        P(None, "tensor", "task"),
        P(None, "task", "tensor"),
    )
    out_specs = P("tensor", "task")
    return jax.shard_map(
        on_device, mesh=mesh, in_specs=in_specs, out_specs=out_specs, check_vma=False
    )
```

```python
import functools

import jax
import jax.numpy as jnp
from jax import lax
from jax.experimental import pallas as pl
from jax.experimental.pallas import tpu as pltpu
from jax.sharding import PartitionSpec as P

F32 = jnp.float32
BF16 = jnp.bfloat16
TASKS = 16
NX, NZ, NC = 4, 4, 2
NQ = NX * NZ
VMEM_BYTES = 48 * 1024 * 1024
INSIDE_BYTES = 24 * 1024 * 1024


def task_of(x, z, c):
    return (x * NZ + z) * NC + c


def task_perm(move):
    pairs = []
    for x in range(NX):
        for z in range(NZ):
            for c in range(NC):
                pairs.append((task_of(x, z, c), task_of(*move(x, z, c))))
    return pairs


CORE = task_perm(lambda x, z, c: (x, z, 1 - c))
TO_X = {d: task_perm(lambda x, z, c, d=d: ((x + d) % NX, z, c)) for d in (1, 2, 3)}
TO_Z = {d: task_perm(lambda x, z, c, d=d: (x, (z + d) % NZ, c)) for d in (1, 2, 3)}
CHIPS = [[task_of(x, z, c) for x in range(NX) for z in range(NZ)] for c in range(NC)]
FAR_FIRST = (2, 1, 3)


def sds(shape, dtype=BF16):
    return jax.ShapeDtypeStruct(shape, dtype)


def whole(a):
    return pl.BlockSpec(a.shape, lambda *_: (0,) * len(a.shape))


def call(kernel, out_shape, *args, scalars, grid=(1,), in_specs=None, out_specs=None, scratch=()):
    many = isinstance(out_shape, (list, tuple))
    if in_specs is None:
        in_specs = [whole(a) for a in args]
    if out_specs is None:
        out_specs = [whole(o) for o in out_shape] if many else whole(out_shape)
    return pl.pallas_call(
        kernel,
        out_shape=out_shape,
        grid_spec=pltpu.PrefetchScalarGridSpec(
            num_scalar_prefetch=1,
            grid=grid,
            in_specs=in_specs,
            out_specs=out_specs,
            scratch_shapes=list(scratch),
        ),
        compiler_params=pltpu.CompilerParams(vmem_limit_bytes=VMEM_BYTES),
    )(scalars, *args)


def call_inside(kernel, out_shape, *args, scalars, hbm=0, scratch=()):
    inside = pl.BlockSpec(memory_space=pltpu.VMEM)
    specs = [pl.BlockSpec(memory_space=pltpu.HBM)] * hbm + [inside] * (len(args) - hbm)
    many = isinstance(out_shape, (list, tuple))
    return pl.pallas_call(
        kernel,
        out_shape=out_shape,
        in_specs=[pl.BlockSpec(memory_space=pltpu.SMEM)] + specs,
        out_specs=[inside] * len(out_shape) if many else inside,
        scratch_shapes=list(scratch),
        compiler_params=pltpu.CompilerParams(vmem_limit_bytes=INSIDE_BYTES),
    )(scalars, *args)


def rows_of(v):
    v = v.astype(F32)
    return v.reshape(v.shape[0] * v.shape[1], v.shape[2])


def latent_kernel(width, s, tokens, low_own, low_other, out):
    c, q = s[2], s[3]
    x = rows_of(tokens[...])
    low = jnp.concatenate([low_own[c], low_other[c], low_other[1 - c], low_own[1 - c]], axis=1)
    lat = jnp.dot(x[:, :width].astype(BF16), low, preferred_element_type=F32)
    tail = x[:, width:]
    lane = lax.broadcasted_iota(jnp.int32, tail.shape, 1)
    weight = jnp.sum(
        jnp.where((lane == q) | (lane == TASKS + q), tail, 0.0), axis=1, keepdims=True
    )
    ranks = lat.shape[1]
    out[:, :ranks] = (lat * weight).astype(BF16)
    feats = out.shape[1] - ranks
    start = pl.multiple_of(lax.rem(q, 2) * feats, feats)
    out[:, ranks:] = rows_of(tokens[:, :, pl.ds(start, feats)]).astype(BF16)


def mid_kernel(ranks, s, got, out):
    c = s[2]
    total = got[0, :, :ranks].astype(F32)
    for j in range(1, got.shape[0]):
        total += got[j, :, :ranks].astype(F32)
    half = (got.shape[2] - ranks) // 2
    own = got[s[3] // 2, :, pl.ds(pl.multiple_of(ranks + c * half, half), half)]
    other = got[s[3] // 2, :, pl.ds(pl.multiple_of(ranks + (1 - c) * half, half), half)]
    for j in range(out.shape[0]):
        out[j, :, :half] = own
        out[j, :, half : 2 * half] = other
        out[j, :, 2 * half :] = total.astype(BF16)


def token_rows(own, other):
    n = own.shape[1] // 4
    a = own[:, : 3 * n]
    b = jnp.concatenate([other[:, n : 2 * n], other[:, :n], other[:, 3 * n :]], axis=1)
    return jnp.concatenate([a, b], axis=0)


def main_kernel(limit, d, s, rows_own, rows_other, w_own, w_other, u_own, u_other, out_a, out_b):
    w = jnp.concatenate([w_own[0], w_other[...], u_own[0], u_other[...]], axis=1)
    rows = token_rows(rows_own, rows_other)
    p = lax.dot_general(w, rows, (((1,), (1,)), ((), ())), preferred_element_type=F32)
    n = p.shape[0]
    at = lax.rem(s[0] + d, NX) * n + lax.broadcasted_iota(jnp.int32, p.shape, 0)
    p = jnp.where(at < limit, p, 0.0)
    m = out_a.shape[1]
    for k, out in enumerate((out_a, out_a, out_b, out_b)):
        out[k % 2] = p[k * m : (k + 1) * m].astype(out.dtype)


def near_kernel(limit, halves, s, rows_own, rows_other, w_own, w_other, u_own, u_other, *outs):
    i = pl.program_id(0)
    w = jnp.concatenate([w_own[0], w_other[...], u_own[0], u_other[...]], axis=1)
    rows = token_rows(rows_own, rows_other)
    p = lax.dot_general(w, rows, (((1,), (1,)), ((), ())), preferred_element_type=F32)
    n = p.shape[0]
    at = half_block(halves, i, s) * n + lax.broadcasted_iota(jnp.int32, p.shape, 0)
    p = jnp.where(at < limit, p, 0.0)
    for k, out in enumerate(outs):

        @pl.when(i == k)
        def _():
            out[0] = p[: n // 2].astype(out.dtype)
            out[1] = p[n // 2 :].astype(out.dtype)


def half_block(halves, i, s):
    (d, h), (e, g) = halves
    return lax.rem(s[0] + jnp.where(i == 0, d, e), NX) * 2 + jnp.where(i == 0, h, g)


def pass_kernel(s, a, got_a, b, got_b, out_a, out_b):
    out_a[...] = (a[...] + got_a[...].astype(F32)).astype(BF16)
    out_b[...] = (b[...] + got_b[...].astype(F32)).astype(BF16)


def x_sum_kernel(s, a0, a1, a2, b0, b1, b2, o0, o1, o2, o3, held):
    for k in range(2):
        held[k] = a0[k] + a1[k].astype(F32) + a2[k].astype(F32)
        held[2 + k] = b0[k] + b1[k].astype(F32) + b2[k].astype(F32)
    for i, o in enumerate((o0, o1, o2, o3)):
        o[...] = held[lax.rem(s[1] + i, NZ)].astype(o.dtype)


def z_sum_kernel(s, a0, a1, a2, a3, keep, send):
    t = a0[...] + a1[...].astype(F32) + a2[...].astype(F32) + a3[...].astype(F32)
    m = keep.shape[1]
    keep[...] = t[:, :m]
    send[...] = t[:, m:]


def silu_kernel(s, keep, got, out):
    first = s[2] == 0
    gate = jnp.where(first, keep[...], got[...])
    up = jnp.where(first, got[...], keep[...])
    out[...] = (gate / (1.0 + jnp.exp(-gate)) * up).astype(BF16)


def stack_kernel(s, h0, h2, h1, h3, out):
    for d, h in enumerate((h0, h1, h2, h3)):
        out[lax.rem(s[1] - d + NZ, NZ)] = h[...]


def down_rows(d, s, h, held, deep_all):
    n, m = h.shape[:2]
    deep = n * m
    held[:16] = jnp.zeros((16, held.shape[1]), F32)
    for k in range(n):
        held[16 + k * m : 16 + (k + 1) * m] = h[k].astype(F32)
    at = lax.rem(s[0] - d + NX, NX)
    shift = jnp.where(at == NX - 1, NX * deep - deep_all, 0)
    t = held[pl.ds(pl.multiple_of(16 - shift, 8), deep)].T.astype(BF16)
    return t, pl.ds(pl.multiple_of(at * deep - shift, 16), deep)


def down_own_kernel(s, w_own, w_other, h, w, out, held, sems):
    cols = w_own.shape[1]
    copies = [
        pltpu.make_async_copy(ref, w.at[:, pl.ds(i * cols, cols)], sems.at[i])
        for i, ref in enumerate((w_own, w_other))
    ]
    for copy in copies:
        copy.start()
    t, at = down_rows(0, s, h, held, w.shape[0])
    for copy in copies:
        copy.wait()
    out[...] = jnp.dot(t, w[at], preferred_element_type=F32)


def down_kernel(s, acc, h2, h1, h3, w, out, held):
    p = acc[...]
    for d, h in enumerate((h1, h2, h3), 1):
        t, at = down_rows(d, s, h, held.at[d - 1], w.shape[0])
        p += jnp.dot(t, w[at], preferred_element_type=F32)
    out[...] = p.astype(BF16).reshape(out.shape)


def tensor_sum_kernel(s, got, keep, send):
    t = got[0].astype(F32)
    for j in range(1, got.shape[0]):
        t += got[j].astype(F32)
    cols = keep.shape[1]
    keep[...] = t[:, :cols]
    send[...] = t[:, cols:]


def place_kernel(s, keep, got, out):
    first = s[2] == 0
    a = jnp.where(first, keep[...], got[...])
    b = jnp.where(first, got[...], keep[...])
    for i in range(out.shape[0] // 16):
        out[16 * i : 16 * i + 8] = a[8 * i : 8 * i + 8]
        out[16 * i + 8 : 16 * i + 16] = b[8 * i : 8 * i + 8]


def on_device(tokens, router, gate_up_weight, down_weight, lower_factor, upper_factor):
    t = lax.axis_index("task").astype(jnp.int32)
    c = lax.rem(t, NC)
    q = t // NC
    x, z = q // NZ, lax.rem(q, NZ)
    s = jnp.stack([x, z, c, q])
    tensor = lax.axis_size("tensor")
    run = functools.partial(call, scalars=s)

    def permute(a, perm):
        return lax.ppermute(a, "task", perm)

    def across(a):
        return lax.all_to_all(a, "tensor", 0, 0)

    def other(a):
        return lax.dynamic_index_in_dim(a, 1 - c, 0, keepdims=False)

    rows, width = tokens.shape
    ranks = 2 * lower_factor.shape[2]
    feats = 2 * gate_up_weight.shape[1]
    hid = gate_up_weight.shape[2]
    count = NQ * NC * rows
    weight = jnp.swapaxes(gate_up_weight, 1, 2)
    upper = jnp.swapaxes(upper_factor, 1, 2)
    zb = -(-hid // (NX * NZ * 8)) * 8
    xb = NZ * zb

    low_other = permute(lower_factor, CORE)
    w_other = permute(other(weight), CORE)
    u_other = permute(other(upper), CORE)
    down_other = permute(down_weight, CORE)

    high = lax.reduce_precision(router, 8, 7)
    fill = jnp.zeros((rows, 128 - 2 * TASKS), BF16)
    packed = jnp.concatenate(
        [tokens, high.astype(BF16), (router - high).astype(BF16), fill], axis=1
    )
    packed = jnp.broadcast_to(packed[None], (NQ,) + packed.shape)
    own_rows = lax.all_to_all(packed, "task", 0, 0, axis_index_groups=CHIPS)
    half = count // 2
    columns = 2 * ranks + feats
    lat = run(
        functools.partial(latent_kernel, width),
        sds((half, columns)),
        own_rows,
        lower_factor,
        low_other,
    )
    got = across(lat.reshape(tensor, half // tensor, columns))
    mid = run(functools.partial(mid_kernel, 2 * ranks), sds(got.shape), got)
    cat = across(mid).reshape(half, columns)
    cat_other = permute(cat, CORE)
    inside = functools.partial(call_inside, scalars=s)

    def product(kernel, block, at, dtype, steps=1):
        def own_spec(a):
            return pl.BlockSpec((1, block, a.shape[2]), lambda i, s: (s[2], at(i, s), 0))

        def spec(a):
            return pl.BlockSpec((block, a.shape[1]), lambda i, s: (at(i, s), 0))

        return run(
            kernel,
            [sds((2, zb, count), dtype)] * 2,
            cat,
            cat_other,
            weight,
            w_other,
            upper,
            u_other,
            grid=(steps,),
            in_specs=[
                whole(cat),
                whole(cat_other),
                own_spec(weight),
                spec(w_other),
                own_spec(upper),
                spec(u_other),
            ],
        )

    def main(d, dtype):
        kernel = functools.partial(main_kernel, hid, d)
        return product(kernel, xb, lambda i, s: lax.rem(s[0] + d, NX), dtype)

    def near(halves, dtype):
        kernel = functools.partial(near_kernel, hid, halves)
        return product(kernel, xb // 2, functools.partial(half_block, halves), dtype, 2)

    far_a, far_b = main(2, BF16)
    far_a = permute(far_a, TO_X[1])
    far_b = permute(far_b, TO_X[3])
    up_b, down_a = near(((1, 1), (3, 0)), BF16)
    up_b = permute(up_b, TO_X[1])
    down_a = permute(down_a, TO_X[3])
    up_a, down_b = near(((1, 0), (3, 1)), F32)
    up_a, down_b = run(pass_kernel, [sds(far_a.shape)] * 2, up_a, far_a, down_b, far_b)
    up_a = permute(up_a, TO_X[1])
    down_b = permute(down_b, TO_X[3])
    own_a, own_b = main(0, F32)
    parts = run(
        x_sum_kernel,
        [sds((zb, count), F32)] + [sds((zb, count))] * 3,
        own_a,
        down_a,
        up_a,
        own_b,
        up_b,
        down_b,
        scratch=[pltpu.VMEM((NZ, zb, count), F32)],
    )
    got = {d: permute(parts[d], TO_Z[d]) for d in FAR_FIRST}
    keep, send = run(
        z_sum_kernel, [sds((zb, count // 2), F32)] * 2, parts[0], got[2], got[1], got[3]
    )
    hidden = run(silu_kernel, sds((zb, count // 2)), keep, permute(send, CORE))

    got = {d: permute(hidden, TO_Z[d]) for d in FAR_FIRST}
    hidden = run(stack_kernel, sds((NZ, zb, count // 2)), hidden, got[2], got[1], got[3])
    got = {d: permute(hidden, TO_X[d]) for d in FAR_FIRST}
    cols = down_weight.shape[1]
    out_rows = count // 2 // tensor
    down, mixed = inside(
        down_own_kernel,
        [sds((hid, 2 * cols)), sds((half, 2 * cols), F32)],
        down_weight,
        down_other,
        hidden,
        hbm=2,
        scratch=[pltpu.VMEM((xb + 16, half), F32), pltpu.SemaphoreType.DMA((2,))],
    )
    mixed = inside(
        down_kernel,
        sds((tensor, out_rows, 2 * cols)),
        mixed,
        got[2],
        got[1],
        got[3],
        down,
        scratch=[pltpu.VMEM((3, xb + 16, half), F32)],
    )
    keep, send = run(tensor_sum_kernel, [sds((out_rows, cols), F32)] * 2, across(mixed))
    return run(place_kernel, sds((2 * out_rows, cols), F32), keep, permute(send, CORE))


def solution(mesh):
    in_specs = (
        P("task", "tensor"),
        P("task", None),
        P(None, "task", "tensor"),
        P("tensor", "task"),
        P(None, "tensor", "task"),
        P(None, "task", "tensor"),
    )
    out_specs = P("tensor", "task")
    return jax.shard_map(
        on_device, mesh=mesh, in_specs=in_specs, out_specs=out_specs, check_vma=False
    )
```

```python
import functools

import jax
import jax.numpy as jnp
from jax import lax
from jax.experimental import pallas as pl
from jax.experimental.pallas import tpu as pltpu
from jax.sharding import PartitionSpec as P

F32 = jnp.float32
BF16 = jnp.bfloat16
TASKS = 16
NX, NZ, NC = 4, 4, 2
NQ = NX * NZ
VMEM_BYTES = 48 * 1024 * 1024
JOIN_BYTES = 46 * 1024 * 1024
INSIDE_BYTES = 24 * 1024 * 1024


def task_of(x, z, c):
    return (x * NZ + z) * NC + c


def task_perm(move):
    pairs = []
    for x in range(NX):
        for z in range(NZ):
            for c in range(NC):
                pairs.append((task_of(x, z, c), task_of(*move(x, z, c))))
    return pairs


CORE = task_perm(lambda x, z, c: (x, z, 1 - c))
TO_X = {d: task_perm(lambda x, z, c, d=d: ((x + d) % NX, z, c)) for d in (1, 2, 3)}
TO_Z = {d: task_perm(lambda x, z, c, d=d: (x, (z + d) % NZ, c)) for d in (1, 2, 3)}
CHIPS = [[task_of(x, z, c) for x in range(NX) for z in range(NZ)] for c in range(NC)]
FAR_FIRST = (2, 1, 3)


def sds(shape, dtype=BF16):
    return jax.ShapeDtypeStruct(shape, dtype)


def whole(a):
    return pl.BlockSpec(a.shape, lambda *_: (0,) * len(a.shape))


def call(kernel, out_shape, *args, scalars, grid=(1,), in_specs=None, out_specs=None, scratch=()):
    many = isinstance(out_shape, (list, tuple))
    if in_specs is None:
        in_specs = [whole(a) for a in args]
    if out_specs is None:
        out_specs = [whole(o) for o in out_shape] if many else whole(out_shape)
    return pl.pallas_call(
        kernel,
        out_shape=out_shape,
        grid_spec=pltpu.PrefetchScalarGridSpec(
            num_scalar_prefetch=1,
            grid=grid,
            in_specs=in_specs,
            out_specs=out_specs,
            scratch_shapes=list(scratch),
        ),
        compiler_params=pltpu.CompilerParams(vmem_limit_bytes=VMEM_BYTES),
    )(scalars, *args)


def call_inside(kernel, out_shape, *args, scalars, hbm=0, scratch=()):
    inside = pl.BlockSpec(memory_space=pltpu.VMEM)
    specs = [pl.BlockSpec(memory_space=pltpu.HBM)] * hbm + [inside] * (len(args) - hbm)
    many = isinstance(out_shape, (list, tuple))
    return pl.pallas_call(
        kernel,
        out_shape=out_shape,
        in_specs=[pl.BlockSpec(memory_space=pltpu.SMEM)] + specs,
        out_specs=[inside] * len(out_shape) if many else inside,
        scratch_shapes=list(scratch),
        compiler_params=pltpu.CompilerParams(vmem_limit_bytes=INSIDE_BYTES),
    )(scalars, *args)


def rows_of(v):
    v = v.astype(F32)
    return v.reshape(v.shape[0] * v.shape[1], v.shape[2])


def latent_kernel(width, s, tokens, low_own, low_other, out):
    c, q = s[2], s[3]
    x = rows_of(tokens[...])
    low = jnp.concatenate([low_own[c], low_other[c], low_other[1 - c], low_own[1 - c]], axis=1)
    lat = jnp.dot(x[:, :width].astype(BF16), low, preferred_element_type=F32)
    tail = x[:, width:]
    lane = lax.broadcasted_iota(jnp.int32, tail.shape, 1)
    weight = jnp.sum(
        jnp.where((lane == q) | (lane == TASKS + q), tail, 0.0), axis=1, keepdims=True
    )
    ranks = lat.shape[1]
    out[:, :ranks] = (lat * weight).astype(BF16)
    feats = out.shape[1] - ranks
    start = pl.multiple_of(lax.rem(q, 2) * feats, feats)
    out[:, ranks:] = rows_of(tokens[:, :, pl.ds(start, feats)]).astype(BF16)


def mid_kernel(ranks, s, got, out):
    c = s[2]
    total = got[0, :, :ranks].astype(F32)
    for j in range(1, got.shape[0]):
        total += got[j, :, :ranks].astype(F32)
    half = (got.shape[2] - ranks) // 2
    own = got[s[3] // 2, :, pl.ds(pl.multiple_of(ranks + c * half, half), half)]
    other = got[s[3] // 2, :, pl.ds(pl.multiple_of(ranks + (1 - c) * half, half), half)]
    for j in range(out.shape[0]):
        out[j, :, :half] = own
        out[j, :, half : 2 * half] = other
        out[j, :, 2 * half :] = total.astype(BF16)


def token_rows(own, other):
    n = own.shape[1] // 4
    a = own[:, : 3 * n]
    b = jnp.concatenate([other[:, n : 2 * n], other[:, :n], other[:, 3 * n :]], axis=1)
    return jnp.concatenate([a, b], axis=0)


def main_kernel(limit, d, s, rows_own, rows_other, w_own, w_other, u_own, u_other, out_a, out_b):
    w = jnp.concatenate([w_own[0], w_other[0], u_own[0], u_other[0]], axis=1)
    rows = token_rows(rows_own, rows_other)
    p = lax.dot_general(w, rows, (((1,), (1,)), ((), ())), preferred_element_type=F32)
    n = p.shape[0]
    at = lax.rem(s[0] + d, NX) * n + lax.broadcasted_iota(jnp.int32, p.shape, 0)
    p = jnp.where(at < limit, p, 0.0)
    m = out_a.shape[1]
    for k, out in enumerate((out_a, out_a, out_b, out_b)):
        out[k % 2] = p[k * m : (k + 1) * m].astype(out.dtype)


def weights_kernel(d, s, w_own, w_other, u_own, u_other, out, sems):
    deep, limit = out.shape[0], w_other.shape[0]
    spare = NX * deep - limit
    copies = []
    start = lax.rem(s[0] + d, NX) * deep
    col = 0
    for n, ref in enumerate((w_own.at[s[2]], w_other, u_own.at[s[2]], u_other)):
        cols = pl.ds(col, ref.shape[1])
        col += ref.shape[1]
        for h, (a, b) in enumerate(((0, deep - spare), (deep - spare, deep))):
            first = jnp.minimum(start + a, limit - (b - a))
            copies.append(
                pltpu.make_async_copy(
                    ref.at[pl.ds(pl.multiple_of(first, 16), b - a)],
                    out.at[pl.ds(a, b - a), cols],
                    sems.at[n, h],
                )
            )
    for copy in copies:
        copy.start()
    for copy in copies:
        copy.wait()


def far_kernel(s, rows_own, rows_other, w, *outs):
    rows = token_rows(rows_own, rows_other)
    p = lax.dot_general(w[...], rows, (((1,), (1,)), ((), ())), preferred_element_type=F32)
    n = outs[0].shape[1]
    for k in range(4):
        outs[k // 2][k % 2] = p[k * n : (k + 1) * n].astype(outs[0].dtype)


def near_kernel(limit, halves, s, rows_own, rows_other, *rest):
    weights, outs = rest[:-2], rest[-2:]
    rows = token_rows(rows_own, rows_other)
    for k, out in enumerate(outs):
        w = jnp.concatenate([weights[2 * i + k][0] for i in range(4)], axis=1)
        p = lax.dot_general(w, rows, (((1,), (1,)), ((), ())), preferred_element_type=F32)
        n = p.shape[0]
        at = half_block(halves[k], s) * n + lax.broadcasted_iota(jnp.int32, p.shape, 0)
        p = jnp.where(at < limit, p, 0.0)
        out[0] = p[: n // 2].astype(out.dtype)
        out[1] = p[n // 2 :].astype(out.dtype)


def half_block(half, s):
    d, h = half
    return lax.rem(s[0] + d, NX) * 2 + h


def pass_kernel(s, a, got_a, b, got_b, out_a, out_b):
    out_a[...] = (a[...] + got_a[...].astype(F32)).astype(BF16)
    out_b[...] = (b[...] + got_b[...].astype(F32)).astype(BF16)


def x_sum_kernel(s, a0, a1, a2, b0, b1, b2, o0, o1, o2, o3, held):
    for k in range(2):
        held[k] = a0[k] + a1[k].astype(F32) + a2[k].astype(F32)
        held[2 + k] = b0[k] + b1[k].astype(F32) + b2[k].astype(F32)
    for i, o in enumerate((o0, o1, o2, o3)):
        o[...] = held[lax.rem(s[1] + i, NZ)].astype(o.dtype)


def z_sum_kernel(s, a0, a1, a2, a3, keep, send):
    t = a0[...] + a1[...].astype(F32) + a2[...].astype(F32) + a3[...].astype(F32)
    m = keep.shape[1]
    keep[...] = t[:, :m]
    send[...] = t[:, m:]


def silu_kernel(s, keep, got, out):
    first = s[2] == 0
    gate = jnp.where(first, keep[...], got[...])
    up = jnp.where(first, got[...], keep[...])
    out[...] = (gate / (1.0 + jnp.exp(-gate)) * up).astype(BF16)


def stack_kernel(s, h0, h2, h1, h3, out):
    for d, h in enumerate((h0, h1, h2, h3)):
        out[lax.rem(s[1] - d + NZ, NZ)] = h[...]


def down_rows(d, s, h, held, deep_all):
    n, m = h.shape[:2]
    deep = n * m
    held[:16] = jnp.zeros((16, held.shape[1]), F32)
    for k in range(n):
        held[16 + k * m : 16 + (k + 1) * m] = h[k].astype(F32)
    at = lax.rem(s[0] - d + NX, NX)
    shift = jnp.where(at == NX - 1, NX * deep - deep_all, 0)
    t = held[pl.ds(pl.multiple_of(16 - shift, 8), deep)].T.astype(BF16)
    return t, pl.ds(pl.multiple_of(at * deep - shift, 16), deep)


def down_own_kernel(s, w_own, w_other, h, w, out, held, sems):
    cols = w_own.shape[1]
    copies = [
        pltpu.make_async_copy(ref, w.at[:, pl.ds(i * cols, cols)], sems.at[i])
        for i, ref in enumerate((w_own, w_other))
    ]
    for copy in copies:
        copy.start()
    t, at = down_rows(0, s, h, held, w.shape[0])
    for copy in copies:
        copy.wait()
    out[...] = jnp.dot(t, w[at], preferred_element_type=F32)


def down_kernel(s, acc, h2, h1, h3, w, out, held):
    p = acc[...]
    for d, h in enumerate((h1, h2, h3), 1):
        t, at = down_rows(d, s, h, held.at[d - 1], w.shape[0])
        p += jnp.dot(t, w[at], preferred_element_type=F32)
    out[...] = p.astype(BF16).reshape(out.shape)


def tensor_sum_kernel(s, got, keep, send):
    t = got[0].astype(F32)
    for j in range(1, got.shape[0]):
        t += got[j].astype(F32)
    cols = keep.shape[1]
    keep[...] = t[:, :cols]
    send[...] = t[:, cols:]


def place_kernel(s, keep, got, out):
    first = s[2] == 0
    a = jnp.where(first, keep[...], got[...])
    b = jnp.where(first, got[...], keep[...])
    for i in range(out.shape[0] // 16):
        out[16 * i : 16 * i + 8] = a[8 * i : 8 * i + 8]
        out[16 * i + 8 : 16 * i + 16] = b[8 * i : 8 * i + 8]


def on_device(tokens, router, gate_up_weight, down_weight, lower_factor, upper_factor):
    t = lax.axis_index("task").astype(jnp.int32)
    c = lax.rem(t, NC)
    q = t // NC
    x, z = q // NZ, lax.rem(q, NZ)
    s = jnp.stack([x, z, c, q])
    tensor = lax.axis_size("tensor")
    run = functools.partial(call, scalars=s)

    def permute(a, perm):
        return lax.ppermute(a, "task", perm)

    def across(a):
        return lax.all_to_all(a, "tensor", 0, 0)

    def other(a):
        return lax.dynamic_index_in_dim(a, 1 - c, 0, keepdims=False)

    rows, width = tokens.shape
    ranks = 2 * lower_factor.shape[2]
    feats = 2 * gate_up_weight.shape[1]
    hid = gate_up_weight.shape[2]
    count = NQ * NC * rows
    weight = jnp.swapaxes(gate_up_weight, 1, 2)
    upper = jnp.swapaxes(upper_factor, 1, 2)
    zb = -(-hid // (NX * NZ * 8)) * 8
    xb = NZ * zb

    low_other = permute(lower_factor, CORE)
    w_other = permute(other(weight), CORE)
    u_other = permute(other(upper), CORE)
    down_other = permute(down_weight, CORE)

    high = lax.reduce_precision(router, 8, 7)
    fill = jnp.zeros((rows, 128 - 2 * TASKS), BF16)
    packed = jnp.concatenate(
        [tokens, high.astype(BF16), (router - high).astype(BF16), fill], axis=1
    )
    packed = jnp.broadcast_to(packed[None], (NQ,) + packed.shape)
    own_rows = lax.all_to_all(packed, "task", 0, 0, axis_index_groups=CHIPS)
    half = count // 2
    columns = 2 * ranks + feats
    lat = run(
        functools.partial(latent_kernel, width),
        sds((half, columns)),
        own_rows,
        lower_factor,
        low_other,
    )
    got = across(lat.reshape(tensor, half // tensor, columns))
    mid = run(functools.partial(mid_kernel, 2 * ranks), sds(got.shape), got)
    cat = across(mid).reshape(half, columns)
    cat_other = permute(cat, CORE)
    inside = functools.partial(call_inside, scalars=s)

    joined = (weight, w_other[None], upper, u_other[None])

    def spec(a, block, at):
        def index(i, s):
            return (s[2] if a.shape[0] > 1 else 0, at(s), 0)

        return pl.BlockSpec((1, block, a.shape[2]), index)

    def product(kernel, specs, args, dtype):
        return run(
            kernel,
            [sds((2, zb, count), dtype)] * 2,
            cat,
            cat_other,
            *args,
            in_specs=[whole(cat), whole(cat_other)] + specs,
        )

    def main(d, dtype):
        specs = [spec(a, xb, lambda s: lax.rem(s[0] + d, NX)) for a in joined]
        return product(functools.partial(main_kernel, hid, d), specs, joined, dtype)

    def near(halves, dtype):
        specs, args = [], []
        for a in joined:
            for half_at in halves:
                specs.append(spec(a, xb // 2, functools.partial(half_block, half_at)))
                args.append(a)
        return product(functools.partial(near_kernel, hid, halves), specs, args, dtype)

    far = pl.pallas_call(
        functools.partial(weights_kernel, 2),
        out_shape=sds((xb, feats + ranks)),
        in_specs=[pl.BlockSpec(memory_space=pltpu.SMEM)]
        + [pl.BlockSpec(memory_space=pl.ANY)] * 4,
        out_specs=pl.BlockSpec(memory_space=pl.ANY),
        scratch_shapes=[pltpu.SemaphoreType.DMA((4, 2))],
        compiler_params=pltpu.CompilerParams(vmem_limit_bytes=JOIN_BYTES),
    )(s, weight, w_other, upper, u_other)
    far_a, far_b = run(far_kernel, [sds((2, zb, count))] * 2, cat, cat_other, far)
    far_a = permute(far_a, TO_X[1])
    far_b = permute(far_b, TO_X[3])
    up_b, down_a = near(((1, 1), (3, 0)), BF16)
    up_b = permute(up_b, TO_X[1])
    down_a = permute(down_a, TO_X[3])
    up_a, down_b = near(((1, 0), (3, 1)), F32)
    up_a, down_b = run(pass_kernel, [sds(far_a.shape)] * 2, up_a, far_a, down_b, far_b)
    up_a = permute(up_a, TO_X[1])
    down_b = permute(down_b, TO_X[3])
    own_a, own_b = main(0, F32)
    parts = run(
        x_sum_kernel,
        [sds((zb, count), F32)] + [sds((zb, count))] * 3,
        own_a,
        down_a,
        up_a,
        own_b,
        up_b,
        down_b,
        scratch=[pltpu.VMEM((NZ, zb, count), F32)],
    )
    got = {d: permute(parts[d], TO_Z[d]) for d in FAR_FIRST}
    keep, send = run(
        z_sum_kernel, [sds((zb, count // 2), F32)] * 2, parts[0], got[2], got[1], got[3]
    )
    hidden = run(silu_kernel, sds((zb, count // 2)), keep, permute(send, CORE))

    got = {d: permute(hidden, TO_Z[d]) for d in FAR_FIRST}
    hidden = run(stack_kernel, sds((NZ, zb, count // 2)), hidden, got[2], got[1], got[3])
    got = {d: permute(hidden, TO_X[d]) for d in FAR_FIRST}
    cols = down_weight.shape[1]
    out_rows = count // 2 // tensor
    down, mixed = inside(
        down_own_kernel,
        [sds((hid, 2 * cols)), sds((half, 2 * cols), F32)],
        down_weight,
        down_other,
        hidden,
        hbm=2,
        scratch=[pltpu.VMEM((xb + 16, half), F32), pltpu.SemaphoreType.DMA((2,))],
    )
    mixed = inside(
        down_kernel,
        sds((tensor, out_rows, 2 * cols)),
        mixed,
        got[2],
        got[1],
        got[3],
        down,
        scratch=[pltpu.VMEM((3, xb + 16, half), F32)],
    )
    keep, send = run(tensor_sum_kernel, [sds((out_rows, cols), F32)] * 2, across(mixed))
    return run(place_kernel, sds((2 * out_rows, cols), F32), keep, permute(send, CORE))


def solution(mesh):
    in_specs = (
        P("task", "tensor"),
        P("task", None),
        P(None, "task", "tensor"),
        P("tensor", "task"),
        P(None, "tensor", "task"),
        P(None, "task", "tensor"),
    )
    out_specs = P("tensor", "task")
    return jax.shard_map(
        on_device, mesh=mesh, in_specs=in_specs, out_specs=out_specs, check_vma=False
    )
```

```python
import functools

import jax
import jax.numpy as jnp
from jax import lax
from jax.experimental import pallas as pl
from jax.experimental.pallas import tpu as pltpu
from jax.sharding import PartitionSpec as P

F32 = jnp.float32
BF16 = jnp.bfloat16
TASKS = 16
NX, NZ, NC = 4, 4, 2
NQ = NX * NZ
VMEM_BYTES = 48 * 1024 * 1024
JOIN_BYTES = 46 * 1024 * 1024
INSIDE_BYTES = 24 * 1024 * 1024


def task_of(x, z, c):
    return (x * NZ + z) * NC + c


def task_perm(move):
    pairs = []
    for x in range(NX):
        for z in range(NZ):
            for c in range(NC):
                pairs.append((task_of(x, z, c), task_of(*move(x, z, c))))
    return pairs


CORE = task_perm(lambda x, z, c: (x, z, 1 - c))
TO_X = {d: task_perm(lambda x, z, c, d=d: ((x + d) % NX, z, c)) for d in (1, 2, 3)}
TO_Z = {d: task_perm(lambda x, z, c, d=d: (x, (z + d) % NZ, c)) for d in (1, 2, 3)}
CHIPS = [[task_of(x, z, c) for x in range(NX) for z in range(NZ)] for c in range(NC)]
FAR_FIRST = (2, 1, 3)


def sds(shape, dtype=BF16):
    return jax.ShapeDtypeStruct(shape, dtype)


def whole(a):
    return pl.BlockSpec(a.shape, lambda *_: (0,) * len(a.shape))


def call(kernel, out_shape, *args, scalars, grid=(1,), in_specs=None, out_specs=None, scratch=()):
    many = isinstance(out_shape, (list, tuple))
    if in_specs is None:
        in_specs = [whole(a) for a in args]
    if out_specs is None:
        out_specs = [whole(o) for o in out_shape] if many else whole(out_shape)
    return pl.pallas_call(
        kernel,
        out_shape=out_shape,
        grid_spec=pltpu.PrefetchScalarGridSpec(
            num_scalar_prefetch=1,
            grid=grid,
            in_specs=in_specs,
            out_specs=out_specs,
            scratch_shapes=list(scratch),
        ),
        compiler_params=pltpu.CompilerParams(vmem_limit_bytes=VMEM_BYTES),
    )(scalars, *args)


def call_inside(kernel, out_shape, *args, scalars, hbm=0, scratch=()):
    inside = pl.BlockSpec(memory_space=pltpu.VMEM)
    specs = [pl.BlockSpec(memory_space=pltpu.HBM)] * hbm + [inside] * (len(args) - hbm)
    many = isinstance(out_shape, (list, tuple))
    return pl.pallas_call(
        kernel,
        out_shape=out_shape,
        in_specs=[pl.BlockSpec(memory_space=pltpu.SMEM)] + specs,
        out_specs=[inside] * len(out_shape) if many else inside,
        scratch_shapes=list(scratch),
        compiler_params=pltpu.CompilerParams(vmem_limit_bytes=INSIDE_BYTES),
    )(scalars, *args)


def rows_of(v):
    v = v.astype(F32)
    return v.reshape(v.shape[0] * v.shape[1], v.shape[2])


def latent_kernel(width, s, own, far, up, down, low_own, low_other, out):
    x, z, c, q = s[0], s[1], s[2], s[3]
    blocks = [ref[...] for ref in (own, far, up, down)]
    tokens = jnp.concatenate([rows_of(b) for b in blocks], axis=0)
    low = jnp.concatenate([low_own[c], low_other[c], low_other[1 - c], low_own[1 - c]], axis=1)
    lat = jnp.dot(tokens[:, :width].astype(BF16), low, preferred_element_type=F32)
    tail = tokens[:, width:]
    lane = lax.broadcasted_iota(jnp.int32, tail.shape, 1)
    weight = jnp.sum(
        jnp.where((lane == q) | (lane == TASKS + q), tail, 0.0), axis=1, keepdims=True
    )
    lat = lat * weight
    n, ranks = own.shape[1], lat.shape[1]
    feats = out.shape[2] - ranks
    start = pl.multiple_of(lax.rem(q, 2) * feats, feats)
    for i, (d, ref) in enumerate(zip((0, 2, 1, 3), (own, far, up, down))):
        for k, e in enumerate((0, 2, 1, 3)):
            at = lax.rem(x - d + NX, NX) * NZ + lax.rem(z - e + NZ, NZ)
            r = (i * NZ + k) * n
            out[at, :, :ranks] = lat[r : r + n].astype(BF16)
            out[at, :, ranks:] = ref[k, :, pl.ds(start, feats)]


def mid_kernel(ranks, s, got, out):
    c = s[2]
    total = got[0, :, :ranks].astype(F32)
    for j in range(1, got.shape[0]):
        total += got[j, :, :ranks].astype(F32)
    half = (got.shape[2] - ranks) // 2
    own = got[s[3] // 2, :, pl.ds(pl.multiple_of(ranks + c * half, half), half)]
    other = got[s[3] // 2, :, pl.ds(pl.multiple_of(ranks + (1 - c) * half, half), half)]
    for j in range(out.shape[0]):
        out[j, :, :half] = own
        out[j, :, half : 2 * half] = other
        out[j, :, 2 * half :] = total.astype(BF16)


def token_rows(own, other):
    n = own.shape[1] // 4
    a = own[:, : 3 * n]
    b = jnp.concatenate([other[:, n : 2 * n], other[:, :n], other[:, 3 * n :]], axis=1)
    return jnp.concatenate([a, b], axis=0)


def main_kernel(limit, d, s, rows_own, rows_other, w_own, w_other, u_own, u_other, out_a, out_b):
    w = jnp.concatenate([w_own[0], w_other[0], u_own[0], u_other[0]], axis=1)
    rows = token_rows(rows_own, rows_other)
    p = lax.dot_general(w, rows, (((1,), (1,)), ((), ())), preferred_element_type=F32)
    n = p.shape[0]
    at = lax.rem(s[0] + d, NX) * n + lax.broadcasted_iota(jnp.int32, p.shape, 0)
    p = jnp.where(at < limit, p, 0.0)
    m = out_a.shape[1]
    for k, out in enumerate((out_a, out_a, out_b, out_b)):
        out[k % 2] = p[k * m : (k + 1) * m].astype(out.dtype)


def weights_kernel(d, s, w_own, w_other, u_own, u_other, out, sems):
    deep, limit = out.shape[0], w_other.shape[0]
    spare = NX * deep - limit
    copies = []
    start = lax.rem(s[0] + d, NX) * deep
    col = 0
    for n, ref in enumerate((w_own.at[s[2]], w_other, u_own.at[s[2]], u_other)):
        cols = pl.ds(col, ref.shape[1])
        col += ref.shape[1]
        for h, (a, b) in enumerate(((0, deep - spare), (deep - spare, deep))):
            first = jnp.minimum(start + a, limit - (b - a))
            copies.append(
                pltpu.make_async_copy(
                    ref.at[pl.ds(pl.multiple_of(first, 16), b - a)],
                    out.at[pl.ds(a, b - a), cols],
                    sems.at[n, h],
                )
            )
    for copy in copies:
        copy.start()
    for copy in copies:
        copy.wait()


def far_kernel(s, rows_own, rows_other, w, *outs):
    rows = token_rows(rows_own, rows_other)
    p = lax.dot_general(w[...], rows, (((1,), (1,)), ((), ())), preferred_element_type=F32)
    n = outs[0].shape[1]
    for k in range(4):
        outs[k // 2][k % 2] = p[k * n : (k + 1) * n].astype(outs[0].dtype)


def near_kernel(limit, halves, s, rows_own, rows_other, *rest):
    weights, outs = rest[:-2], rest[-2:]
    rows = token_rows(rows_own, rows_other)
    for k, out in enumerate(outs):
        w = jnp.concatenate([weights[2 * i + k][0] for i in range(4)], axis=1)
        p = lax.dot_general(w, rows, (((1,), (1,)), ((), ())), preferred_element_type=F32)
        n = p.shape[0]
        at = half_block(halves[k], s) * n + lax.broadcasted_iota(jnp.int32, p.shape, 0)
        p = jnp.where(at < limit, p, 0.0)
        out[0] = p[: n // 2].astype(out.dtype)
        out[1] = p[n // 2 :].astype(out.dtype)


def half_block(half, s):
    d, h = half
    return lax.rem(s[0] + d, NX) * 2 + h


def pass_kernel(s, a, got_a, b, got_b, out_a, out_b):
    out_a[...] = (a[...] + got_a[...].astype(F32)).astype(BF16)
    out_b[...] = (b[...] + got_b[...].astype(F32)).astype(BF16)


def x_sum_kernel(s, a0, a1, a2, b0, b1, b2, o0, o1, o2, o3, held):
    for k in range(2):
        held[k] = a0[k] + a1[k].astype(F32) + a2[k].astype(F32)
        held[2 + k] = b0[k] + b1[k].astype(F32) + b2[k].astype(F32)
    for i, o in enumerate((o0, o1, o2, o3)):
        o[...] = held[lax.rem(s[1] + i, NZ)].astype(o.dtype)


def z_sum_kernel(s, a0, a1, a2, a3, keep, send):
    t = a0[...] + a1[...].astype(F32) + a2[...].astype(F32) + a3[...].astype(F32)
    m = keep.shape[1]
    keep[...] = t[:, :m]
    send[...] = t[:, m:]


def silu_kernel(s, keep, got, out):
    first = s[2] == 0
    gate = jnp.where(first, keep[...], got[...])
    up = jnp.where(first, got[...], keep[...])
    out[...] = (gate / (1.0 + jnp.exp(-gate)) * up).astype(BF16)


def stack_kernel(s, h0, h2, h1, h3, out):
    for d, h in enumerate((h0, h1, h2, h3)):
        out[lax.rem(s[1] - d + NZ, NZ)] = h[...]


def down_rows(d, s, h, held, deep_all):
    n, m = h.shape[:2]
    deep = n * m
    held[:16] = jnp.zeros((16, held.shape[1]), F32)
    for k in range(n):
        held[16 + k * m : 16 + (k + 1) * m] = h[k].astype(F32)
    at = lax.rem(s[0] - d + NX, NX)
    shift = jnp.where(at == NX - 1, NX * deep - deep_all, 0)
    t = held[pl.ds(pl.multiple_of(16 - shift, 8), deep)].T.astype(BF16)
    return t, pl.ds(pl.multiple_of(at * deep - shift, 16), deep)


def down_own_kernel(s, w_own, w_other, h, w, out, held, sems):
    cols = w_own.shape[1]
    copies = [
        pltpu.make_async_copy(ref, w.at[:, pl.ds(i * cols, cols)], sems.at[i])
        for i, ref in enumerate((w_own, w_other))
    ]
    for copy in copies:
        copy.start()
    t, at = down_rows(0, s, h, held, w.shape[0])
    for copy in copies:
        copy.wait()
    out[...] = jnp.dot(t, w[at], preferred_element_type=F32)


def down_kernel(s, acc, h2, h1, h3, w, out, held):
    p = acc[...]
    for d, h in enumerate((h1, h2, h3), 1):
        t, at = down_rows(d, s, h, held.at[d - 1], w.shape[0])
        p += jnp.dot(t, w[at], preferred_element_type=F32)
    out[...] = p.astype(BF16).reshape(out.shape)


def tensor_sum_kernel(s, got, keep, send):
    t = got[0].astype(F32)
    for j in range(1, got.shape[0]):
        t += got[j].astype(F32)
    cols = keep.shape[1]
    keep[...] = t[:, :cols]
    send[...] = t[:, cols:]


def place_kernel(s, keep, got, out):
    first = s[2] == 0
    a = jnp.where(first, keep[...], got[...])
    b = jnp.where(first, got[...], keep[...])
    for i in range(out.shape[0] // 16):
        out[16 * i : 16 * i + 8] = a[8 * i : 8 * i + 8]
        out[16 * i + 8 : 16 * i + 16] = b[8 * i : 8 * i + 8]


def on_device(tokens, router, gate_up_weight, down_weight, lower_factor, upper_factor):
    t = lax.axis_index("task").astype(jnp.int32)
    c = lax.rem(t, NC)
    q = t // NC
    x, z = q // NZ, lax.rem(q, NZ)
    s = jnp.stack([x, z, c, q])
    tensor = lax.axis_size("tensor")
    run = functools.partial(call, scalars=s)

    def permute(a, perm):
        return lax.ppermute(a, "task", perm)

    def across(a):
        return lax.all_to_all(a, "tensor", 0, 0)

    def other(a):
        return lax.dynamic_index_in_dim(a, 1 - c, 0, keepdims=False)

    rows, width = tokens.shape
    ranks = 2 * lower_factor.shape[2]
    feats = 2 * gate_up_weight.shape[1]
    hid = gate_up_weight.shape[2]
    count = NQ * NC * rows
    weight = jnp.swapaxes(gate_up_weight, 1, 2)
    upper = jnp.swapaxes(upper_factor, 1, 2)
    zb = -(-hid // (NX * NZ * 8)) * 8
    xb = NZ * zb

    low_other = permute(lower_factor, CORE)
    u_branch = other(upper)
    down_other = permute(down_weight, CORE)

    high = lax.reduce_precision(router, 8, 7)
    fill = jnp.zeros((rows, 128 - 2 * TASKS), BF16)
    packed = jnp.concatenate(
        [tokens, high.astype(BF16), (router - high).astype(BF16), fill], axis=1
    )
    got = [permute(packed, TO_Z[d]) for d in FAR_FIRST]
    packed = jnp.stack([packed] + got)
    packed, w_late = lax.optimization_barrier((packed, weight))
    w_branch = other(w_late)
    got = [permute(packed, TO_X[d]) for d in FAR_FIRST]
    half = count // 2
    columns = 2 * ranks + feats
    lat = run(
        functools.partial(latent_kernel, width),
        sds((NQ, rows, columns)),
        packed,
        *got,
        lower_factor,
        low_other,
    )
    lat, w_branch, u_branch = lax.optimization_barrier((lat, w_branch, u_branch))
    w_other = permute(w_branch, CORE)
    u_other = permute(u_branch, CORE)
    got = across(lat.reshape(tensor, half // tensor, columns))
    mid = run(functools.partial(mid_kernel, 2 * ranks), sds(got.shape), got)
    cat = across(mid).reshape(half, columns)
    cat_other = permute(cat, CORE)
    inside = functools.partial(call_inside, scalars=s)

    joined = (weight, w_other[None], upper, u_other[None])

    def spec(a, block, at):
        def index(i, s):
            return (s[2] if a.shape[0] > 1 else 0, at(s), 0)

        return pl.BlockSpec((1, block, a.shape[2]), index)

    def product(kernel, specs, args, dtype):
        return run(
            kernel,
            [sds((2, zb, count), dtype)] * 2,
            cat,
            cat_other,
            *args,
            in_specs=[whole(cat), whole(cat_other)] + specs,
        )

    def main(d, dtype):
        specs = [spec(a, xb, lambda s: lax.rem(s[0] + d, NX)) for a in joined]
        return product(functools.partial(main_kernel, hid, d), specs, joined, dtype)

    def near(halves, dtype):
        specs, args = [], []
        for a in joined:
            for half_at in halves:
                specs.append(spec(a, xb // 2, functools.partial(half_block, half_at)))
                args.append(a)
        return product(functools.partial(near_kernel, hid, halves), specs, args, dtype)

    far = pl.pallas_call(
        functools.partial(weights_kernel, 2),
        out_shape=sds((xb, feats + ranks)),
        in_specs=[pl.BlockSpec(memory_space=pltpu.SMEM)]
        + [pl.BlockSpec(memory_space=pl.ANY)] * 4,
        out_specs=pl.BlockSpec(memory_space=pl.ANY),
        scratch_shapes=[pltpu.SemaphoreType.DMA((4, 2))],
        compiler_params=pltpu.CompilerParams(vmem_limit_bytes=JOIN_BYTES),
    )(s, weight, w_other, upper, u_other)
    far_a, far_b = run(far_kernel, [sds((2, zb, count))] * 2, cat, cat_other, far)
    far_a = permute(far_a, TO_X[1])
    far_b = permute(far_b, TO_X[3])
    up_b, down_a = near(((1, 1), (3, 0)), BF16)
    up_b = permute(up_b, TO_X[1])
    down_a = permute(down_a, TO_X[3])
    up_a, down_b = near(((1, 0), (3, 1)), F32)
    up_a, down_b = run(pass_kernel, [sds(far_a.shape)] * 2, up_a, far_a, down_b, far_b)
    up_a = permute(up_a, TO_X[1])
    down_b = permute(down_b, TO_X[3])
    own_a, own_b = main(0, F32)
    parts = run(
        x_sum_kernel,
        [sds((zb, count), F32)] + [sds((zb, count))] * 3,
        own_a,
        down_a,
        up_a,
        own_b,
        up_b,
        down_b,
        scratch=[pltpu.VMEM((NZ, zb, count), F32)],
    )
    got = {d: permute(parts[d], TO_Z[d]) for d in FAR_FIRST}
    keep, send = run(
        z_sum_kernel, [sds((zb, count // 2), F32)] * 2, parts[0], got[2], got[1], got[3]
    )
    hidden = run(silu_kernel, sds((zb, count // 2)), keep, permute(send, CORE))

    got = {d: permute(hidden, TO_Z[d]) for d in FAR_FIRST}
    hidden = run(stack_kernel, sds((NZ, zb, count // 2)), hidden, got[2], got[1], got[3])
    got = {d: permute(hidden, TO_X[d]) for d in FAR_FIRST}
    cols = down_weight.shape[1]
    out_rows = count // 2 // tensor
    down, mixed = inside(
        down_own_kernel,
        [sds((hid, 2 * cols)), sds((half, 2 * cols), F32)],
        down_weight,
        down_other,
        hidden,
        hbm=2,
        scratch=[pltpu.VMEM((xb + 16, half), F32), pltpu.SemaphoreType.DMA((2,))],
    )
    mixed = inside(
        down_kernel,
        sds((tensor, out_rows, 2 * cols)),
        mixed,
        got[2],
        got[1],
        got[3],
        down,
        scratch=[pltpu.VMEM((3, xb + 16, half), F32)],
    )
    keep, send = run(tensor_sum_kernel, [sds((out_rows, cols), F32)] * 2, across(mixed))
    return run(place_kernel, sds((2 * out_rows, cols), F32), keep, permute(send, CORE))


def solution(mesh):
    in_specs = (
        P("task", "tensor"),
        P("task", None),
        P(None, "task", "tensor"),
        P("tensor", "task"),
        P(None, "tensor", "task"),
        P(None, "task", "tensor"),
    )
    out_specs = P("tensor", "task")
    return jax.shard_map(
        on_device, mesh=mesh, in_specs=in_specs, out_specs=out_specs, check_vma=False
    )
```

```python
import functools

import jax
import jax.numpy as jnp
from jax import lax
from jax.experimental import pallas as pl
from jax.experimental.pallas import tpu as pltpu
from jax.sharding import PartitionSpec as P

F32 = jnp.float32
BF16 = jnp.bfloat16
TASKS = 16
NX, NZ, NC = 4, 4, 2
NQ = NX * NZ
VMEM_BYTES = 48 * 1024 * 1024
JOIN_BYTES = 46 * 1024 * 1024
INSIDE_BYTES = 24 * 1024 * 1024


def task_of(x, z, c):
    return (x * NZ + z) * NC + c


def task_perm(move):
    pairs = []
    for x in range(NX):
        for z in range(NZ):
            for c in range(NC):
                pairs.append((task_of(x, z, c), task_of(*move(x, z, c))))
    return pairs


CORE = task_perm(lambda x, z, c: (x, z, 1 - c))
TO_X = {d: task_perm(lambda x, z, c, d=d: ((x + d) % NX, z, c)) for d in (1, 2, 3)}
TO_Z = {d: task_perm(lambda x, z, c, d=d: (x, (z + d) % NZ, c)) for d in (1, 2, 3)}
CHIPS = [[task_of(x, z, c) for x in range(NX) for z in range(NZ)] for c in range(NC)]
FAR_FIRST = (2, 1, 3)


def sds(shape, dtype=BF16):
    return jax.ShapeDtypeStruct(shape, dtype)


def whole(a):
    return pl.BlockSpec(a.shape, lambda *_: (0,) * len(a.shape))


def call(kernel, out_shape, *args, scalars, grid=(1,), in_specs=None, out_specs=None, scratch=()):
    many = isinstance(out_shape, (list, tuple))
    if in_specs is None:
        in_specs = [whole(a) for a in args]
    if out_specs is None:
        out_specs = [whole(o) for o in out_shape] if many else whole(out_shape)
    return pl.pallas_call(
        kernel,
        out_shape=out_shape,
        grid_spec=pltpu.PrefetchScalarGridSpec(
            num_scalar_prefetch=1,
            grid=grid,
            in_specs=in_specs,
            out_specs=out_specs,
            scratch_shapes=list(scratch),
        ),
        compiler_params=pltpu.CompilerParams(vmem_limit_bytes=VMEM_BYTES),
    )(scalars, *args)


def call_inside(kernel, out_shape, *args, scalars, hbm=0, scratch=()):
    inside = pl.BlockSpec(memory_space=pltpu.VMEM)
    specs = [pl.BlockSpec(memory_space=pltpu.HBM)] * hbm + [inside] * (len(args) - hbm)
    many = isinstance(out_shape, (list, tuple))
    return pl.pallas_call(
        kernel,
        out_shape=out_shape,
        in_specs=[pl.BlockSpec(memory_space=pltpu.SMEM)] + specs,
        out_specs=[inside] * len(out_shape) if many else inside,
        scratch_shapes=list(scratch),
        compiler_params=pltpu.CompilerParams(vmem_limit_bytes=INSIDE_BYTES),
    )(scalars, *args)


def rows_of(v):
    v = v.astype(F32)
    return v.reshape(v.shape[0] * v.shape[1], v.shape[2])


def latent_kernel(width, s, own, far, up, down, low_own, low_other, out):
    x, z, c, q = s[0], s[1], s[2], s[3]
    blocks = [ref[...] for ref in (own, far, up, down)]
    tokens = jnp.concatenate([rows_of(b) for b in blocks], axis=0)
    low = jnp.concatenate([low_own[c], low_other[c], low_other[1 - c], low_own[1 - c]], axis=1)
    lat = jnp.dot(tokens[:, :width].astype(BF16), low, preferred_element_type=F32)
    tail = tokens[:, width:]
    lane = lax.broadcasted_iota(jnp.int32, tail.shape, 1)
    weight = jnp.sum(
        jnp.where((lane == q) | (lane == TASKS + q), tail, 0.0), axis=1, keepdims=True
    )
    lat = lat * weight
    n, ranks = own.shape[1], lat.shape[1]
    feats = out.shape[2] - ranks
    start = pl.multiple_of(lax.rem(q, 2) * feats, feats)
    for i, (d, ref) in enumerate(zip((0, 2, 1, 3), (own, far, up, down))):
        for k, e in enumerate((0, 2, 1, 3)):
            at = lax.rem(x - d + NX, NX) * NZ + lax.rem(z - e + NZ, NZ)
            r = (i * NZ + k) * n
            out[at, :, :ranks] = lat[r : r + n].astype(BF16)
            out[at, :, ranks:] = ref[k, :, pl.ds(start, feats)]


def mid_kernel(ranks, s, got, out):
    c = s[2]
    total = got[0, :, :ranks].astype(F32)
    for j in range(1, got.shape[0]):
        total += got[j, :, :ranks].astype(F32)
    half = (got.shape[2] - ranks) // 2
    own = got[s[3] // 2, :, pl.ds(pl.multiple_of(ranks + c * half, half), half)]
    other = got[s[3] // 2, :, pl.ds(pl.multiple_of(ranks + (1 - c) * half, half), half)]
    for j in range(out.shape[0]):
        out[j, :, :half] = own
        out[j, :, half : 2 * half] = other
        out[j, :, 2 * half :] = total.astype(BF16)


def token_rows(own, other):
    n = own.shape[1] // 4
    a = own[:, : 3 * n]
    b = jnp.concatenate([other[:, n : 2 * n], other[:, :n], other[:, 3 * n :]], axis=1)
    return jnp.concatenate([a, b], axis=0)


def main_kernel(limit, d, s, rows_own, rows_other, w_own, w_other, u_own, u_other, out_a, out_b):
    w = jnp.concatenate([w_own[0], w_other[0], u_own[0], u_other[0]], axis=1)
    rows = token_rows(rows_own, rows_other)
    p = lax.dot_general(w, rows, (((1,), (1,)), ((), ())), preferred_element_type=F32)
    n = p.shape[0]
    at = lax.rem(s[0] + d, NX) * n + lax.broadcasted_iota(jnp.int32, p.shape, 0)
    p = jnp.where(at < limit, p, 0.0)
    m = out_a.shape[1]
    for k, out in enumerate((out_a, out_a, out_b, out_b)):
        out[k % 2] = p[k * m : (k + 1) * m].astype(out.dtype)


def weights_kernel(d, s, w_own, w_other, u_own, u_other, out, sems):
    deep, limit = out.shape[0], w_other.shape[0]
    spare = NX * deep - limit
    copies = []
    start = lax.rem(s[0] + d, NX) * deep
    col = 0
    for n, ref in enumerate((w_own.at[s[2]], w_other, u_own.at[s[2]], u_other)):
        cols = pl.ds(col, ref.shape[1])
        col += ref.shape[1]
        for h, (a, b) in enumerate(((0, deep - spare), (deep - spare, deep))):
            first = jnp.minimum(start + a, limit - (b - a))
            copies.append(
                pltpu.make_async_copy(
                    ref.at[pl.ds(pl.multiple_of(first, 16), b - a)],
                    out.at[pl.ds(a, b - a), cols],
                    sems.at[n, h],
                )
            )
    for copy in copies:
        copy.start()
    for copy in copies:
        copy.wait()


def far_kernel(s, rows_own, rows_other, w, *outs):
    rows = token_rows(rows_own, rows_other)
    p = lax.dot_general(w[...], rows, (((1,), (1,)), ((), ())), preferred_element_type=F32)
    n = outs[0].shape[1]
    for k in range(4):
        outs[k // 2][k % 2] = p[k * n : (k + 1) * n].astype(outs[0].dtype)


def near_kernel(limit, halves, s, rows_own, rows_other, *rest):
    weights, outs = rest[:-2], rest[-2:]
    rows = token_rows(rows_own, rows_other)
    for k, out in enumerate(outs):
        w = jnp.concatenate([weights[2 * i + k][0] for i in range(4)], axis=1)
        p = lax.dot_general(w, rows, (((1,), (1,)), ((), ())), preferred_element_type=F32)
        n = p.shape[0]
        at = half_block(halves[k], s) * n + lax.broadcasted_iota(jnp.int32, p.shape, 0)
        p = jnp.where(at < limit, p, 0.0)
        out[0] = p[: n // 2].astype(out.dtype)
        out[1] = p[n // 2 :].astype(out.dtype)


def half_block(half, s):
    d, h = half
    return lax.rem(s[0] + d, NX) * 2 + h


def pass_kernel(s, a, got_a, b, got_b, out_a, out_b):
    out_a[...] = (a[...] + got_a[...].astype(F32)).astype(BF16)
    out_b[...] = (b[...] + got_b[...].astype(F32)).astype(BF16)


def x_sum_kernel(s, a0, a1, a2, b0, b1, b2, o0, o1, o2, o3, held):
    for k in range(2):
        held[k] = a0[k] + a1[k].astype(F32) + a2[k].astype(F32)
        held[2 + k] = b0[k] + b1[k].astype(F32) + b2[k].astype(F32)
    for i, o in enumerate((o0, o1, o2, o3)):
        o[...] = held[lax.rem(s[1] + i, NZ)].astype(o.dtype)


def z_sum_kernel(s, a0, a1, a2, a3, keep, send):
    t = a0[...] + a1[...].astype(F32) + a2[...].astype(F32) + a3[...].astype(F32)
    m = keep.shape[1]
    keep[...] = t[:, :m]
    send[...] = t[:, m:]


def silu_kernel(s, keep, got, out):
    first = s[2] == 0
    gate = jnp.where(first, keep[...], got[...])
    up = jnp.where(first, got[...], keep[...])
    out[...] = (gate / (1.0 + jnp.exp(-gate)) * up).astype(BF16)


def stack_kernel(s, h0, h2, h1, h3, out):
    for d, h in enumerate((h0, h1, h2, h3)):
        out[lax.rem(s[1] - d + NZ, NZ)] = h[...]


def down_rows(d, s, h, held, deep_all):
    n, m = h.shape[:2]
    deep = n * m
    held[:16] = jnp.zeros((16, held.shape[1]), F32)
    for k in range(n):
        held[16 + k * m : 16 + (k + 1) * m] = h[k].astype(F32)
    at = lax.rem(s[0] - d + NX, NX)
    shift = jnp.where(at == NX - 1, NX * deep - deep_all, 0)
    t = held[pl.ds(pl.multiple_of(16 - shift, 8), deep)].T.astype(BF16)
    return t, pl.ds(pl.multiple_of(at * deep - shift, 16), deep)


def down_own_kernel(s, w_own, w_other, h, w, out, held, sems):
    cols = w_own.shape[1]
    copies = [
        pltpu.make_async_copy(ref, w.at[:, pl.ds(i * cols, cols)], sems.at[i])
        for i, ref in enumerate((w_own, w_other))
    ]
    for copy in copies:
        copy.start()
    t, at = down_rows(0, s, h, held, w.shape[0])
    for copy in copies:
        copy.wait()
    out[...] = jnp.dot(t, w[at], preferred_element_type=F32)


def down_kernel(s, acc, h2, h1, h3, w, out, held):
    p = acc[...]
    for d, h in enumerate((h1, h2, h3), 1):
        t, at = down_rows(d, s, h, held.at[d - 1], w.shape[0])
        p += jnp.dot(t, w[at], preferred_element_type=F32)
    out[...] = p.astype(BF16).reshape(out.shape)


def tensor_sum_kernel(s, got, keep, send):
    t = got[0].astype(F32)
    for j in range(1, got.shape[0]):
        t += got[j].astype(F32)
    cols = keep.shape[1]
    keep[...] = t[:, :cols]
    send[...] = t[:, cols:]


def place_kernel(s, keep, got, out):
    first = s[2] == 0
    a = jnp.where(first, keep[...], got[...])
    b = jnp.where(first, got[...], keep[...])
    for i in range(out.shape[0] // 16):
        out[16 * i : 16 * i + 8] = a[8 * i : 8 * i + 8]
        out[16 * i + 8 : 16 * i + 16] = b[8 * i : 8 * i + 8]


def on_device(tokens, router, gate_up_weight, down_weight, lower_factor, upper_factor):
    t = lax.axis_index("task").astype(jnp.int32)
    c = lax.rem(t, NC)
    q = t // NC
    x, z = q // NZ, lax.rem(q, NZ)
    s = jnp.stack([x, z, c, q])
    tensor = lax.axis_size("tensor")
    run = functools.partial(call, scalars=s)

    def permute(a, perm):
        return lax.ppermute(a, "task", perm)

    def across(a):
        return lax.all_to_all(a, "tensor", 0, 0)

    def other(a):
        return lax.dynamic_index_in_dim(a, 1 - c, 0, keepdims=False)

    rows, width = tokens.shape
    ranks = 2 * lower_factor.shape[2]
    feats = 2 * gate_up_weight.shape[1]
    hid = gate_up_weight.shape[2]
    count = NQ * NC * rows
    weight = jnp.swapaxes(gate_up_weight, 1, 2)
    upper = jnp.swapaxes(upper_factor, 1, 2)
    zb = -(-hid // (NX * NZ * 8)) * 8
    xb = NZ * zb

    low_other = permute(lower_factor, CORE)
    down_other = permute(down_weight, CORE)

    high = lax.reduce_precision(router, 8, 7)
    fill = jnp.zeros((rows, 128 - 2 * TASKS), BF16)
    packed = jnp.concatenate(
        [tokens, high.astype(BF16), (router - high).astype(BF16), fill], axis=1
    )
    got = [permute(packed, TO_Z[d]) for d in FAR_FIRST]
    packed = jnp.stack([packed] + got)
    packed, w_late = lax.optimization_barrier((packed, weight))
    w_branch = other(w_late)
    got = [permute(packed, TO_X[d]) for d in FAR_FIRST]
    half = count // 2
    columns = 2 * ranks + feats
    lat = run(
        functools.partial(latent_kernel, width),
        sds((NQ, rows, columns)),
        packed,
        *got,
        lower_factor,
        low_other,
    )
    lat, w_branch, u_late = lax.optimization_barrier((lat, w_branch, upper))
    w_other = permute(w_branch, CORE)
    u_other = permute(other(u_late), CORE)
    got = across(lat.reshape(tensor, half // tensor, columns))
    mid = run(functools.partial(mid_kernel, 2 * ranks), sds(got.shape), got)
    cat = across(mid).reshape(half, columns)
    cat_other = permute(cat, CORE)
    inside = functools.partial(call_inside, scalars=s)

    joined = (weight, w_other[None], upper, u_other[None])

    def spec(a, block, at):
        def index(i, s):
            return (s[2] if a.shape[0] > 1 else 0, at(s), 0)

        return pl.BlockSpec((1, block, a.shape[2]), index)

    def product(kernel, specs, args, dtype):
        return run(
            kernel,
            [sds((2, zb, count), dtype)] * 2,
            cat,
            cat_other,
            *args,
            in_specs=[whole(cat), whole(cat_other)] + specs,
        )

    def main(d, dtype):
        specs = [spec(a, xb, lambda s: lax.rem(s[0] + d, NX)) for a in joined]
        return product(functools.partial(main_kernel, hid, d), specs, joined, dtype)

    def near(halves, dtype):
        specs, args = [], []
        for a in joined:
            for half_at in halves:
                specs.append(spec(a, xb // 2, functools.partial(half_block, half_at)))
                args.append(a)
        return product(functools.partial(near_kernel, hid, halves), specs, args, dtype)

    far = pl.pallas_call(
        functools.partial(weights_kernel, 2),
        out_shape=sds((xb, feats + ranks)),
        in_specs=[pl.BlockSpec(memory_space=pltpu.SMEM)]
        + [pl.BlockSpec(memory_space=pl.ANY)] * 4,
        out_specs=pl.BlockSpec(memory_space=pl.ANY),
        scratch_shapes=[pltpu.SemaphoreType.DMA((4, 2))],
        compiler_params=pltpu.CompilerParams(vmem_limit_bytes=JOIN_BYTES),
    )(s, weight, w_other, upper, u_other)
    far_a, far_b = run(far_kernel, [sds((2, zb, count))] * 2, cat, cat_other, far)
    far_a = permute(far_a, TO_X[1])
    far_b = permute(far_b, TO_X[3])
    up_b, down_a = near(((1, 1), (3, 0)), BF16)
    up_b = permute(up_b, TO_X[1])
    down_a = permute(down_a, TO_X[3])
    up_a, down_b = near(((1, 0), (3, 1)), F32)
    up_a, down_b = run(pass_kernel, [sds(far_a.shape)] * 2, up_a, far_a, down_b, far_b)
    up_a = permute(up_a, TO_X[1])
    down_b = permute(down_b, TO_X[3])
    own_a, own_b = main(0, F32)
    parts = run(
        x_sum_kernel,
        [sds((zb, count), F32)] + [sds((zb, count))] * 3,
        own_a,
        down_a,
        up_a,
        own_b,
        up_b,
        down_b,
        scratch=[pltpu.VMEM((NZ, zb, count), F32)],
    )
    got = {d: permute(parts[d], TO_Z[d]) for d in FAR_FIRST}
    keep, send = run(
        z_sum_kernel, [sds((zb, count // 2), F32)] * 2, parts[0], got[2], got[1], got[3]
    )
    hidden = run(silu_kernel, sds((zb, count // 2)), keep, permute(send, CORE))

    got = {d: permute(hidden, TO_Z[d]) for d in FAR_FIRST}
    hidden = run(stack_kernel, sds((NZ, zb, count // 2)), hidden, got[2], got[1], got[3])
    got = {d: permute(hidden, TO_X[d]) for d in FAR_FIRST}
    cols = down_weight.shape[1]
    out_rows = count // 2 // tensor
    down, mixed = inside(
        down_own_kernel,
        [sds((hid, 2 * cols)), sds((half, 2 * cols), F32)],
        down_weight,
        down_other,
        hidden,
        hbm=2,
        scratch=[pltpu.VMEM((xb + 16, half), F32), pltpu.SemaphoreType.DMA((2,))],
    )
    mixed = inside(
        down_kernel,
        sds((tensor, out_rows, 2 * cols)),
        mixed,
        got[2],
        got[1],
        got[3],
        down,
        scratch=[pltpu.VMEM((3, xb + 16, half), F32)],
    )
    keep, send = run(tensor_sum_kernel, [sds((out_rows, cols), F32)] * 2, across(mixed))
    return run(place_kernel, sds((2 * out_rows, cols), F32), keep, permute(send, CORE))


def solution(mesh):
    in_specs = (
        P("task", "tensor"),
        P("task", None),
        P(None, "task", "tensor"),
        P("tensor", "task"),
        P(None, "tensor", "task"),
        P(None, "task", "tensor"),
    )
    out_specs = P("tensor", "task")
    return jax.shard_map(
        on_device, mesh=mesh, in_specs=in_specs, out_specs=out_specs, check_vma=False
    )
```
